32 devices in a mesh: gx: 4 (over y, x), gz: 8 (over z, core).
Axes of the slice: x: 2, y: 2, z: 4, core: 2. Of those that a mesh axis runs over, the one named last changes fastest.
Arguments:
- adjoint: float32 [3, 128, 64, 512], P(None, 'gz', 'gx')
- base_flow: float32 [2, 128, 64, 512], P(None, 'gz', 'gx'), may hold values from 0.5 to 1.5
- conductance: float32 [128, 64, 512], P('gz', 'gx'), may hold values from 20 to 80
- ground_mask: int32 [64, 512], P('gx'), may hold values 0 or 1
- turbine_cells: int32 [3, 100], replicated, may hold values from 0 to 511, as said below
- yaw_bin: int32 [100], replicated, may hold values from 0 to 11
- yaw_table: float32 [3, 12], replicated, may hold values from -20 to 20
Outputs:
- adjoint_out: float32 [3, 128, 64, 512], P(None, 'gz', 'gx')
The draws below stay inside these ranges and needn't reach their ends.
Inputs may be any that keep to these rules, and one draw needn't show every extreme that they name: `turbine_cells`: row 0 holds a turbine's vertical cell, below 128; row 1 its streamwise cell, below 64; row 2 its spanwise cell, below 512. Turbines may share a cell. Some turbine stands in the cell (0, 0, 0) and some in the cell (127, 63, 511).
All inputs are finite; a program needn't handle non-finite values. No bound on the sum of `ground_mask` on one device may be relied on, other than what follows from the above.
Results may differ from the reference program's by a relative error of at most 0.0003.
Values sent between devices are 32-bit elements; how exact they have to be, the bound alone decides.
No kernel may reach another device: no remote copies, remote signals or barrier semaphores. Data moves between devices by JAX's collectives and lax.ppermute only.
A program may use at most 192 MiB of HBM per device.

```python
import math
import jax
import jax.numpy as jnp
from jax import lax

SWEEPS = 2
TURB = 100
BINS = 12
NX = 64
NY = 512
NZ = 128


def draw_adjoint(key, part):
    first_key, second_key = jax.random.split(jax.random.fold_in(key, 11))
    column_part = jax.random.normal(first_key, (3, 1, NX, NY), jnp.float32)
    cell_part = 0.3 * jax.random.normal(second_key, (3, NZ, NX, NY), jnp.float32)
    return column_part + cell_part


def draw_turbine_cells(key, part):
    base_key = jax.random.fold_in(key, 23)
    z_key, x_key, y_key = jax.random.split(base_key, 3)
    vertical = jax.random.randint(z_key, (TURB,), 0, NZ, jnp.int32)
    streamwise = jax.random.randint(x_key, (TURB,), 0, NX, jnp.int32)
    spanwise = jax.random.randint(y_key, (TURB,), 0, NY, jnp.int32)
    vertical = vertical.at[0].set(NZ - 1).at[1].set(0)
    streamwise = streamwise.at[0].set(NX - 1).at[1].set(0)
    spanwise = spanwise.at[0].set(NY - 1).at[1].set(0)
    return jnp.stack([vertical, streamwise, spanwise], 0)


def touch_ends(values, stream_key, low, largest):
    place = [jax.random.randint(jax.random.fold_in(stream_key, axis), (), 0, length) for axis, length in enumerate(values.shape)]
    longest = values.shape.index(max(values.shape))
    next_to = place[:longest] + [(place[longest] + 1) % values.shape[longest]] + place[longest + 1:]
    return values.at[tuple(place)].set(low).at[tuple(next_to)].set(largest)


def block_scale(rng, shape, cuts, smallest, largest):
    gain = 1.0
    for axis_at, blocks in cuts:
        draws = jax.random.uniform(jax.random.fold_in(jax.random.fold_in(rng, 6), axis_at), (blocks,), jnp.float32, smallest / len(cuts), largest / len(cuts))
        gain = gain * jnp.repeat(jnp.exp(draws), shape[axis_at] // blocks).reshape((-1,) + (1,) * (len(shape) - 1 - axis_at))
    return gain


def bell_draw(key, shape, scale, most, held_as=jnp.bfloat16):
    return jnp.clip(scale * jax.random.normal(key, shape, jnp.float32), -most, most).astype(held_as)


def setup_inputs(seed: int = 0) -> dict:
    seeds = jax.random.split(jax.random.key(seed), 8)
    adjoint = draw_adjoint(jax.random.fold_in(seeds[7], 71), 0)
    base_flow = jnp.clip(0.5 + 1.0 * jax.random.uniform(seeds[1], (2, NZ, NX, NY), jnp.float32) ** block_scale(seeds[1], (2, NZ, NX, NY), ((1, 8), (2, 4)), -0.2, 0.2), 0.5, 1.5)
    conductance = jnp.clip(jnp.exp(math.log(80.0) - 1.3862944 * jax.random.uniform(seeds[2], (NZ, NX, NY), jnp.float32) ** block_scale(seeds[2], (NZ, NX, NY), ((0, 8), (1, 4)), -0.2, 0.2)), 20.0, 80.0)
    ground_mask = touch_ends((jax.random.randint(seeds[3], (NX, NY), 0, 2) < 1).astype(jnp.int32), jax.random.fold_in(seeds[3], 1), 0, 1)
    turbine_cells = draw_turbine_cells(jax.random.fold_in(seeds[7], 71), 0)
    yaw_bin = touch_ends(jax.random.randint(seeds[5], (TURB,), 0, BINS), jax.random.fold_in(seeds[5], 1), 0, BINS - 1).astype(jnp.int32)
    yaw_table = bell_draw(seeds[6], (3, BINS), 5.0, 20.0, jnp.float32)
    return {"adjoint": adjoint, "base_flow": base_flow, "conductance": conductance, "ground_mask": ground_mask, "turbine_cells": turbine_cells, "yaw_bin": yaw_bin, "yaw_table": yaw_table}


PSEUDO_STEP = 0.2
LATERAL_VISC = 1.0


def thomas(sub_diag, main_diag, super_diag, right_side):
    def forward(carry, row_values):
        ratio_prev, value_prev = carry
        lower_c, centre, upper_c, target = row_values
        pivot = centre - lower_c * ratio_prev
        ratio_next = upper_c / pivot
        value_next = (target - lower_c * value_prev) / pivot
        return (ratio_next, value_next), (ratio_next, value_next)

    start = (jnp.zeros(super_diag.shape[1:], jnp.float32), jnp.zeros(right_side.shape[1:], jnp.float32))
    _, (ratios, values) = lax.scan(forward, start, (sub_diag, main_diag, super_diag, right_side))

    def backward(later, row_values):
        ratio_here, value_here = row_values
        result = value_here - ratio_here * later
        return result, result

    _, solved = lax.scan(backward, jnp.zeros(right_side.shape[1:], jnp.float32), (ratios, values), reverse=True)
    return solved


def lateral(adjoint_now, base_flow, x_minus, x_plus):
    padded_y = jnp.pad(adjoint_now, ((0, 0), (0, 0), (0, 0), (1, 1)))
    y_minus = padded_y[:, :, :, :-2]
    y_plus = padded_y[:, :, :, 2:]
    advect = base_flow[0:1] * (x_plus - x_minus) * 0.5 + base_flow[1:2] * (y_plus - y_minus) * 0.5
    spread = x_plus + x_minus + y_plus + y_minus - 4.0 * adjoint_now
    return adjoint_now + PSEUDO_STEP * (advect + LATERAL_VISC * spread)


def reference(adjoint, base_flow, conductance, ground_mask, turbine_cells, yaw_bin, yaw_table):
    z_cells = adjoint.shape[1]
    columns = adjoint.shape[2] * adjoint.shape[3]
    strengths = yaw_table[:, yaw_bin]
    source = jnp.zeros(adjoint.shape, jnp.float32).at[:, turbine_cells[0], turbine_cells[1], turbine_cells[2]].add(strengths)
    cond_cols = conductance.reshape(z_cells, columns)
    wall_flag = ground_mask.reshape(columns).astype(jnp.float32)
    low_face = jnp.concatenate([(cond_cols[0] * wall_flag)[None], cond_cols[1:]], 0)
    zero_row = jnp.zeros((1, columns), jnp.float32)
    sub_diag = jnp.concatenate([zero_row, -cond_cols[1:]], 0)
    super_diag = jnp.concatenate([-cond_cols[1:], zero_row], 0)
    main_diag = 1.0 + low_face + jnp.concatenate([cond_cols[1:], zero_row], 0)
    current = adjoint
    for sweep_index in range(SWEEPS):
        padded_x = jnp.pad(current, ((0, 0), (0, 0), (1, 1), (0, 0)))
        right_side = lateral(current, base_flow, padded_x[:, :, :-2], padded_x[:, :, 2:]) + source
        stacked = jnp.moveaxis(right_side.reshape(3, z_cells, columns), 1, 0)
        solved = thomas(sub_diag[:, None], main_diag[:, None], super_diag[:, None], stacked)
        current = jnp.moveaxis(solved, 0, 1).reshape(adjoint.shape)
    return current
```

```python
import functools

import jax
import jax.numpy as jnp
from jax import lax
from jax.experimental import pallas as pl
from jax.experimental.pallas import tpu as pltpu
from jax.sharding import PartitionSpec as P

SWEEPS = 2
PSEUDO_STEP = 0.2
LATERAL_VISC = 1.0


F32 = jnp.float32
VMEM = pl.BlockSpec(memory_space=pltpu.VMEM)
SMEM = pl.BlockSpec(memory_space=pltpu.SMEM)
PARAMS = pltpu.CompilerParams(vmem_limit_bytes=48 * 1024 * 1024)


def call(body, outs, ins, specs=None, scratch=()):
    return pl.pallas_call(
        body,
        out_shape=[jax.ShapeDtypeStruct(s, F32) for s in outs],
        in_specs=specs or [VMEM] * len(ins),
        out_specs=[VMEM] * len(outs),
        scratch_shapes=list(scratch),
        compiler_params=PARAMS,
    )(*ins)


def slab_kernel(
    cells_ref, bin_ref, table_ref, cond_ref,
    source_ref, ratio_ref, recip_ref, bottom_ref, top_ref, keep_ref, send_ref,
):
    nz, nx, ny = cond_ref.shape
    z0 = lax.axis_index("gz") * nz
    x0 = lax.axis_index("gx") * nx
    half = lax.rem(lax.axis_index("gz"), 2)
    source_ref[...] = jnp.zeros(source_ref.shape, F32)
    lanes = lax.broadcasted_iota(jnp.int32, (1, ny), 1)

    def place(t, carry):
        lz = cells_ref[0, t] - z0
        lx = cells_ref[1, t] - x0
        inside = (lz >= 0) & (lz < nz) & (lx >= 0) & (lx < nx)

        @pl.when(inside)
        def _():
            here = lanes == cells_ref[2, t]
            for c in range(3):
                row = source_ref[c, lz, pl.ds(lx, 1), :]
                source_ref[c, lz, pl.ds(lx, 1), :] = row + jnp.where(
                    here, table_ref[c, bin_ref[t]], 0.0
                )

        return carry

    lax.fori_loop(0, cells_ref.shape[1], place, 0)

    ends = []
    for tile in range(2):
        rows = pl.ds(tile * 8, 8)
        sigma = jnp.ones((8, ny), F32)
        ratios = [None]
        for k in range(nz - 1):
            face = cond_ref[k + 1, rows, :]
            recip = 1.0 / (sigma + face)
            ratio = face * recip
            recip_ref[k, rows, :] = recip
            ratio_ref[k + 1, rows, :] = ratio
            sigma = 1.0 + sigma * ratio
            ratios.append(ratio)
        weight = 1.0 / sigma
        recip_ref[nz - 1, rows, :] = weight
        ratio_ref[0, rows, :] = jnp.zeros((8, ny), F32)
        top = weight
        top_ref[nz - 1, rows, :] = weight
        for k in range(nz - 2, -1, -1):
            weight = weight * ratios[k + 1]
            top_ref[k, rows, :] = weight
        cross = weight
        tau = jnp.ones((8, ny), F32)
        ratios = [None] * nz
        for k in range(nz - 2, -1, -1):
            face = cond_ref[k + 1, rows, :]
            ratios[k] = face / (tau + face)
            tau = 1.0 + tau * ratios[k]
        weight = 1.0 / tau
        bottom = weight
        bottom_ref[0, rows, :] = weight
        for k in range(nz - 1):
            weight = weight * ratios[k]
            bottom_ref[k + 1, rows, :] = weight
        ends.append((bottom + 1.0 / cond_ref[0, rows, :], cross, top))
    for i in range(3):
        keep_ref[i] = jnp.where(half == 0, ends[0][i], ends[1][i])
        send_ref[i] = jnp.where(half == 0, ends[1][i], ends[0][i])


def right_kernel(
    state_ref, flow_ref, source_ref, ratio_ref, recip_ref, halo_a_ref, halo_b_ref,
    solved_ref, keep_ref, send_ref,
):
    _, nz, nx, ny = state_ref.shape
    strip = lax.axis_index("gx")
    even = lax.rem(strip, 2) == 0
    half = lax.rem(lax.axis_index("gz"), 2)
    inner = ((strip > 0) & (strip < lax.axis_size("gx") - 1)).astype(F32)
    lanes = lax.broadcasted_iota(jnp.int32, (nx, ny), 1)
    rows = lax.broadcasted_iota(jnp.int32, (nx, ny), 0)
    values = [None] * 3
    for k in range(nz):
        u = 0.5 * PSEUDO_STEP * flow_ref[0, k]
        v = 0.5 * PSEUDO_STEP * flow_ref[1, k]
        visc = PSEUDO_STEP * LATERAL_VISC
        x_plus_w = visc + u
        x_minus_w = visc - u
        y_plus_w = jnp.where(lanes == ny - 1, 0.0, visc + v)
        y_minus_w = jnp.where(lanes == 0, 0.0, visc - v)
        ratio = ratio_ref[k]
        for c in range(3):
            a = state_ref[c, k]
            halo_a = halo_a_ref[c, k : k + 1, :]
            halo_b = halo_b_ref[c, k : k + 1, :] * inner
            left = jnp.where(even, halo_b, halo_a)
            right = jnp.where(even, halo_a, halo_b)
            x_minus = jnp.where(rows == 0, left, pltpu.roll(a, 1, 0))
            x_plus = jnp.where(rows == nx - 1, right, pltpu.roll(a, nx - 1, 0))
            y_minus = pltpu.roll(a, 1, 1)
            y_plus = pltpu.roll(a, ny - 1, 1)
            value = (
                (1.0 - 4.0 * visc) * a
                + x_plus_w * x_plus
                + x_minus_w * x_minus
                + y_plus_w * y_plus
                + y_minus_w * y_minus
                + source_ref[c, k]
            )
            if k:
                value = value + ratio * values[c]
            values[c] = value
            solved_ref[c, k] = value
    for k in range(nz - 1, -1, -1):
        recip = recip_ref[k]
        for c in range(3):
            value = solved_ref[c, k] * recip
            if k < nz - 1:
                value = value + ratio_ref[k + 1] * values[c]
            else:
                last = value
                keep_ref[3 + c] = jnp.where(half == 0, last[:8], last[8:])
                send_ref[3 + c] = jnp.where(half == 0, last[8:], last[:8])
            values[c] = value
            solved_ref[c, k] = value
    for c in range(3):
        first = values[c]
        keep_ref[c] = jnp.where(half == 0, first[:8], first[8:])
        send_ref[c] = jnp.where(half == 0, first[8:], first[:8])


def own_pair(half, keep_ref, recv_ref, i):
    mine, other = keep_ref[i], recv_ref[i]
    return jnp.where(half == 0, mine, other), jnp.where(half == 0, other, mine)


def chip_kernel(coef_keep, coef_recv, keep, recv, out_ref, mid_ref):
    half = lax.rem(lax.axis_index("gz"), 2)
    a0, a1 = own_pair(half, coef_keep, coef_recv, 0)
    c0, c1 = own_pair(half, coef_keep, coef_recv, 1)
    d0, d1 = own_pair(half, coef_keep, coef_recv, 2)
    inv = 1.0 / (d0 + a1)
    out_ref[6] = a0 - c0 * c0 * inv
    out_ref[7] = c0 * c1 * inv
    out_ref[8] = d1 - c1 * c1 * inv
    mid_ref[0] = inv
    mid_ref[1] = c0
    mid_ref[2] = c1
    for c in range(3):
        first0, first1 = own_pair(half, keep, recv, c)
        last0, last1 = own_pair(half, keep, recv, 3 + c)
        gap = last0 - first1
        current = gap * inv
        out_ref[c] = first0 - c0 * current
        out_ref[3 + c] = last1 + c1 * current
        mid_ref[3 + c] = current


def join_kernel(chips, *refs):
    own_ref, others = refs[0], refs[1:chips]
    mid_ref, mask_ref = refs[chips : chips + 2]
    keep_ref, send_ref, below_ref, above_ref, own_out, all_ref = refs[chips + 2 :]
    index = lax.axis_index("gz")
    chip, half = lax.div(index, 2), lax.rem(index, 2)
    all_ref[chip] = own_ref[...]
    for j in range(1, chips):
        all_ref[chip ^ j] = others[j - 1][...]
    mask = mask_ref[...].astype(F32)
    mask = jnp.where(half == 0, mask[:8], mask[8:])
    zero = jnp.zeros(mask.shape, F32)

    volt, imp = [zero] * 3, zero
    for t in range(chips - 1):
        inv = 1.0 / (all_ref[t, 6] + imp)
        if t == 0:
            inv = inv * mask
        cross = all_ref[t, 7]
        kappa = cross * inv
        below_ref[t] = kappa
        use = t < chip
        volt = [
            jnp.where(use, all_ref[t, 3 + c] + kappa * (volt[c] - all_ref[t, c]), volt[c])
            for c in range(3)
        ]
        imp = jnp.where(use, all_ref[t, 8] - kappa * cross, imp)
    low_volt, low_imp = volt, imp

    volt, imp = [zero] * 3, zero
    for t in range(chips - 1, 0, -1):
        cross = all_ref[t, 7]
        if t == chips - 1:
            kappa = zero
        else:
            kappa = cross / (all_ref[t, 8] + imp)
        above_ref[t] = kappa
        use = t > chip
        volt = [
            jnp.where(use, all_ref[t, c] + kappa * (volt[c] - all_ref[t, 3 + c]), volt[c])
            for c in range(3)
        ]
        imp = jnp.where(use, all_ref[t, 6] - kappa * cross, imp)
    high_volt, high_imp = volt, imp

    cross, near, far = own_ref[7], own_ref[6], own_ref[8]
    bottom_on = jnp.where(chip == 0, mask, 1.0)
    top_on = jnp.where(chip == chips - 1, 0.0, 1.0)
    up = cross * bottom_on / (near + low_imp)
    down = cross * top_on / (far + high_imp)
    bottom_g = bottom_on / (low_imp + near - down * cross)
    top_g = top_on / (high_imp + far - up * cross)
    own_out[0] = up
    own_out[1] = down
    own_out[2] = bottom_g
    own_out[3] = top_g
    inv, c0, c1 = mid_ref[0], mid_ref[1], mid_ref[2]
    for c in range(3):
        first, last = own_ref[c], own_ref[3 + c]
        j_bottom = (low_volt[c] - first - down * (high_volt[c] - last)) * bottom_g
        j_top = (last + up * (low_volt[c] - first) - high_volt[c]) * top_g
        j_mid = mid_ref[3 + c] + (c0 * j_bottom + c1 * j_top) * inv
        keep_ref[c] = jnp.where(half == 0, j_bottom, j_mid)
        keep_ref[3 + c] = jnp.where(half == 0, j_mid, j_top)
        send_ref[c] = jnp.where(half == 0, j_mid, j_bottom)
        send_ref[3 + c] = jnp.where(half == 0, j_top, j_mid)


def chip_again_kernel(chips, keep, recv, mid_ref, own_coef, *outs):
    volt_ref, parts = outs[0], outs[1:]
    index = lax.axis_index("gz")
    chip, half = lax.div(index, 2), lax.rem(index, 2)
    inv, c0, c1 = mid_ref[0], mid_ref[1], mid_ref[2]
    up, down = own_coef[0], own_coef[1]
    for c in range(3):
        first0, first1 = own_pair(half, keep, recv, c)
        last0, last1 = own_pair(half, keep, recv, 3 + c)
        current = (last0 - first1) * inv
        first = first0 - c0 * current
        last = last1 + c1 * current
        volt_ref[c] = first
        volt_ref[3 + c] = last
        volt_ref[6 + c] = current
        to_above = last - up * first
        to_below = first - down * last
        for j in range(1, chips):
            parts[j - 1][c] = jnp.where((chip ^ j) > chip, to_above, to_below)


def join_again_kernel(chips, *refs):
    others = refs[: chips - 1]
    volt_ref, mid_ref, below_ref, above_ref, own_coef = refs[chips - 1 : chips + 4]
    keep_ref, send_ref, all_ref = refs[chips + 4 :]
    index = lax.axis_index("gz")
    chip, half = lax.div(index, 2), lax.rem(index, 2)
    for j in range(1, chips):
        all_ref[chip ^ j] = others[j - 1][...]
    inv, c0, c1 = mid_ref[0], mid_ref[1], mid_ref[2]
    up, down, bottom_g, top_g = (own_coef[i] for i in range(4))
    for c in range(3):
        low = jnp.zeros(inv.shape, F32)
        for t in range(chips - 1):
            low = jnp.where(t < chip, all_ref[t, c] + below_ref[t] * low, low)
        high = jnp.zeros(inv.shape, F32)
        for t in range(chips - 1, 0, -1):
            high = jnp.where(t > chip, all_ref[t, c] + above_ref[t] * high, high)
        first, last = volt_ref[c], volt_ref[3 + c]
        j_bottom = (low - first - down * (high - last)) * bottom_g
        j_top = (last + up * (low - first) - high) * top_g
        j_mid = volt_ref[6 + c] + (c0 * j_bottom + c1 * j_top) * inv
        keep_ref[c] = jnp.where(half == 0, j_bottom, j_mid)
        keep_ref[3 + c] = jnp.where(half == 0, j_mid, j_top)
        send_ref[c] = jnp.where(half == 0, j_mid, j_bottom)
        send_ref[3 + c] = jnp.where(half == 0, j_top, j_mid)


def update_kernel(solved_ref, bottom_ref, top_ref, keep_ref, recv_ref, *outs):
    out_ref = outs[0]
    _, nz, nx, ny = solved_ref.shape
    half = lax.rem(lax.axis_index("gz"), 2)
    even = lax.rem(lax.axis_index("gx"), 2) == 0
    for c in range(3):
        j_bottom = jnp.concatenate(own_pair(half, keep_ref, recv_ref, c), 0)
        j_top = jnp.concatenate(own_pair(half, keep_ref, recv_ref, 3 + c), 0)
        for k in range(nz):
            value = solved_ref[c, k] + bottom_ref[k] * j_bottom - top_ref[k] * j_top
            out_ref[c, k] = value
            if len(outs) > 1:
                first, last = value[0:1], value[nx - 1 : nx]
                outs[1][c, k : k + 1, :] = jnp.where(even, last, first)
                outs[2][c, k : k + 1, :] = jnp.where(even, first, last)


def per_device(strips, slabs, adjoint, base_flow, conductance, ground_mask, turbine_cells, yaw_bin, yaw_table):
    _, nz, nx, ny = adjoint.shape
    chips = slabs // 2
    cube, field = (nz, nx, ny), adjoint.shape
    pair_a = [(i, i ^ 1) for i in range(strips)]
    pair_b = [((i + 1) % strips, ((i ^ 1) + 1) % strips) for i in range(strips)]
    cores = [(i, i ^ 1) for i in range(slabs)]

    def across(parts):
        return [
            lax.ppermute(part, "gz", [(i, i ^ (2 * (j + 1))) for i in range(slabs)])
            for j, part in enumerate(parts)
        ]

    odd = lax.rem(lax.axis_index("gx"), 2)
    edge_a = lax.dynamic_index_in_dim(adjoint, (1 - odd) * (nx - 1), 2, keepdims=False)
    edge_b = lax.dynamic_index_in_dim(adjoint, odd * (nx - 1), 2, keepdims=False)
    part = lambda n: (n, 8, ny)
    source, ratio, recip, bottom_w, top_w, coef_keep, coef_send = call(
        slab_kernel,
        [field, cube, cube, cube, cube, part(3), part(3)],
        (turbine_cells, yaw_bin, yaw_table, conductance),
        [SMEM, SMEM, SMEM, VMEM],
    )
    coef_recv = lax.ppermute(coef_send, "gz", cores)
    state = adjoint
    for sweep_index in range(SWEEPS):
        halo_a = lax.ppermute(edge_a, "gx", pair_a)
        halo_b = lax.ppermute(edge_b, "gx", pair_b)
        solved, keep, send = call(
            right_kernel,
            [field, part(6), part(6)],
            (state, base_flow, source, ratio, recip, halo_a, halo_b),
        )
        recv = lax.ppermute(send, "gz", cores)
        if sweep_index == 0:
            own, mid = call(chip_kernel, [part(9), part(6)], (coef_keep, coef_recv, keep, recv))
            others = across([own] * (chips - 1))
            j_keep, j_send, below, above, own_coef = call(
                functools.partial(join_kernel, chips),
                [part(6), part(6), (chips, 8, ny), (chips, 8, ny), part(4)],
                (own, *others, mid, ground_mask),
                scratch=[pltpu.VMEM((chips, 9, 8, ny), F32)],
            )
        else:
            volts, *parts = call(
                functools.partial(chip_again_kernel, chips),
                [part(9)] + [part(3)] * (chips - 1),
                (keep, recv, mid, own_coef),
            )
            others = across(parts)
            j_keep, j_send = call(
                functools.partial(join_again_kernel, chips),
                [part(6), part(6)],
                (*others, volts, mid, below, above, own_coef),
                scratch=[pltpu.VMEM((chips, 3, 8, ny), F32)],
            )
        j_recv = lax.ppermute(j_send, "gz", cores)
        last = sweep_index == SWEEPS - 1
        edges = [] if last else [(3, nz, ny)] * 2
        state, *edges = call(
            update_kernel, [field, *edges], (solved, bottom_w, top_w, j_keep, j_recv)
        )
        if not last:
            edge_a, edge_b = edges
    return state


def solution(mesh):
    in_specs = (
        P(None, "gz", "gx", None),
        P(None, "gz", "gx", None),
        P("gz", "gx", None),
        P("gx", None),
        P(),
        P(),
        P(),
    )
    out_specs = P(None, "gz", "gx", None)
    body = functools.partial(per_device, mesh.shape["gx"], mesh.shape["gz"])
    return jax.shard_map(body, mesh=mesh, in_specs=in_specs, out_specs=out_specs, check_vma=False)
```

```python
import functools

import jax
import jax.numpy as jnp
from jax import lax
from jax.experimental import pallas as pl
from jax.experimental.pallas import tpu as pltpu
from jax.sharding import PartitionSpec as P

SWEEPS = 2
PSEUDO_STEP = 0.2
LATERAL_VISC = 1.0


F32 = jnp.float32
EARLY = True
AFTER_EDGE = lambda x: [x]
AFTER_SOURCE = lambda x: [x]
VMEM = pl.BlockSpec(memory_space=pltpu.VMEM)
SMEM = pl.BlockSpec(memory_space=pltpu.SMEM)
ANY = pl.BlockSpec(memory_space=pl.ANY)
PARAMS = pltpu.CompilerParams(vmem_limit_bytes=12 * 1024 * 1024)


def call(body, outs, ins, cost_us, specs=None, scratch=(), after=()):
    def run(*refs):
        body(*refs[: len(ins)], *refs[len(ins) + len(after) :])

    return pl.pallas_call(
        run,
        out_shape=[jax.ShapeDtypeStruct(s, F32) for s in outs],
        in_specs=(specs or [VMEM] * len(ins)) + [ANY] * len(after),
        out_specs=[VMEM] * len(outs),
        scratch_shapes=list(scratch),
        compiler_params=PARAMS,
        cost_estimate=pl.CostEstimate(
            flops=0, bytes_accessed=int(cost_us * 3.0e6), transcendentals=0
        ),
    )(*ins, *after)


def edge_kernel(state_ref, edge_a_ref, edge_b_ref):
    _, nz, nx, _ = state_ref.shape
    even = lax.rem(lax.axis_index("gx"), 2) == 0
    for c in range(3):
        for k in range(nz):
            first, last = state_ref[c, k, 0:1, :], state_ref[c, k, nx - 1 : nx, :]
            edge_a_ref[c, k : k + 1, :] = jnp.where(even, last, first)
            edge_b_ref[c, k : k + 1, :] = jnp.where(even, first, last)


def source_kernel(cells_ref, bin_ref, table_ref, source_ref):
    _, nz, nx, ny = source_ref.shape
    z0 = lax.axis_index("gz") * nz
    x0 = lax.axis_index("gx") * nx
    source_ref[...] = jnp.zeros(source_ref.shape, F32)
    lanes = lax.broadcasted_iota(jnp.int32, (1, ny), 1)

    def place(t, carry):
        lz = cells_ref[0, t] - z0
        lx = cells_ref[1, t] - x0
        inside = (lz >= 0) & (lz < nz) & (lx >= 0) & (lx < nx)

        @pl.when(inside)
        def _():
            here = lanes == cells_ref[2, t]
            for c in range(3):
                row = source_ref[c, lz, pl.ds(lx, 1), :]
                source_ref[c, lz, pl.ds(lx, 1), :] = row + jnp.where(
                    here, table_ref[c, bin_ref[t]], 0.0
                )

        return carry

    lax.fori_loop(0, cells_ref.shape[1], place, 0)


def slab_kernel(cond_ref, ratio_ref, recip_ref, bottom_ref, top_ref, keep_ref, send_ref):
    nz, nx, ny = cond_ref.shape
    half = lax.rem(lax.axis_index("gz"), 2)
    ends = []
    for tile in range(2):
        rows = pl.ds(tile * 8, 8)
        sigma = jnp.ones((8, ny), F32)
        tau = jnp.ones((8, ny), F32)
        for k in range(nz - 1):
            face = cond_ref[k + 1, rows, :]
            recip = 1.0 / (sigma + face)
            ratio = face * recip
            recip_ref[k, rows, :] = recip
            ratio_ref[k + 1, rows, :] = ratio
            sigma = 1.0 + sigma * ratio
            face = cond_ref[nz - 1 - k, rows, :]
            ratio = face / (tau + face)
            bottom_ref[nz - 1 - k, rows, :] = ratio
            tau = 1.0 + tau * ratio
        weight = 1.0 / sigma
        recip_ref[nz - 1, rows, :] = weight
        ratio_ref[0, rows, :] = jnp.zeros((8, ny), F32)
        top = weight
        top_ref[nz - 1, rows, :] = weight
        for k in range(nz - 2, -1, -1):
            weight = weight * ratio_ref[k + 1, rows, :]
            top_ref[k, rows, :] = weight
        cross = weight
        weight = 1.0 / tau
        bottom = weight
        bottom_ref[0, rows, :] = weight
        for k in range(1, nz):
            weight = weight * bottom_ref[k, rows, :]
            bottom_ref[k, rows, :] = weight
        ends.append((bottom + 1.0 / cond_ref[0, rows, :], cross, top))
    for i in range(3):
        keep_ref[i] = jnp.where(half == 0, ends[0][i], ends[1][i])
        send_ref[i] = jnp.where(half == 0, ends[1][i], ends[0][i])


def right_kernel(
    state_ref, flow_ref, source_ref, ratio_ref, recip_ref, bottom_ref, top_ref,
    solved_ref, ends_ref, *edge_refs,
):
    _, nz, nx, ny = state_ref.shape
    lanes = lax.broadcasted_iota(jnp.int32, (nx, ny), 1)
    rows = lax.broadcasted_iota(jnp.int32, (nx, ny), 0)
    visc = PSEUDO_STEP * LATERAL_VISC
    values = [None] * 3
    for k in range(nz):
        u = 0.5 * PSEUDO_STEP * flow_ref[0, k]
        v = 0.5 * PSEUDO_STEP * flow_ref[1, k]
        x_plus_w = visc + u
        x_minus_w = visc - u
        if edge_refs:
            edge_w, end_w = edge_refs
            for side, weight in ((0, x_minus_w[0:1]), (1, x_plus_w[nx - 1 : nx])):
                row = pl.ds(side * (nx - 1), 1)
                edge_w[side, k : k + 1, :] = weight
                end_w[side, 0, k : k + 1, :] = weight * bottom_ref[k, row, :]
                end_w[side, 1, k : k + 1, :] = weight * top_ref[k, row, :]
        x_plus_w = jnp.where(rows == nx - 1, 0.0, x_plus_w)
        x_minus_w = jnp.where(rows == 0, 0.0, x_minus_w)
        y_plus_w = jnp.where(lanes == ny - 1, 0.0, visc + v)
        y_minus_w = jnp.where(lanes == 0, 0.0, visc - v)
        ratio = ratio_ref[k]
        for c in range(3):
            a = state_ref[c, k]
            value = (
                (1.0 - 4.0 * visc) * a
                + x_plus_w * pltpu.roll(a, nx - 1, 0)
                + x_minus_w * pltpu.roll(a, 1, 0)
                + y_plus_w * pltpu.roll(a, ny - 1, 1)
                + y_minus_w * pltpu.roll(a, 1, 1)
                + source_ref[c, k]
            )
            if k:
                value = value + ratio * values[c]
            values[c] = value
            solved_ref[c, k] = value
    for k in range(nz - 1, -1, -1):
        recip = recip_ref[k]
        for c in range(3):
            value = solved_ref[c, k] * recip
            if k < nz - 1:
                value = value + ratio_ref[k + 1] * values[c]
            else:
                ends_ref[3 + c] = value
            values[c] = value
            solved_ref[c, k] = value
    for c in range(3):
        ends_ref[c] = values[c]


def halo_sides(halo_a_ref, halo_b_ref, c):
    strip = lax.axis_index("gx")
    even = lax.rem(strip, 2) == 0
    inner = ((strip > 0) & (strip < lax.axis_size("gx") - 1)).astype(F32)
    halo_a, halo_b = halo_a_ref[c], halo_b_ref[c] * inner
    return jnp.where(even, halo_b, halo_a), jnp.where(even, halo_a, halo_b)


def ends_kernel(ends_ref, halo_a_ref, halo_b_ref, end_w, keep_ref, send_ref):
    half = lax.rem(lax.axis_index("gz"), 2)
    rows = lax.broadcasted_iota(jnp.int32, (8, ends_ref.shape[2]), 0)
    for c in range(3):
        left, right = halo_sides(halo_a_ref, halo_b_ref, c)
        for e in range(2):
            low = jnp.sum(left * end_w[0, e], 0, keepdims=True)
            high = jnp.sum(right * end_w[1, e], 0, keepdims=True)
            i = 3 * e + c
            low = ends_ref[i, 0:8, :] + jnp.where(rows == 0, low, 0.0)
            high = ends_ref[i, 8:16, :] + jnp.where(rows == 7, high, 0.0)
            keep_ref[i] = jnp.where(half == 0, low, high)
            send_ref[i] = jnp.where(half == 0, high, low)


def halo_kernel(solved_ref, halo_a_ref, halo_b_ref, edge_w, ratio_ref, recip_ref, out_ref, right_ref):
    _, nz, nx, ny = solved_ref.shape
    rows = lax.broadcasted_iota(jnp.int32, (8, ny), 0)
    for c in range(3):
        for side, halo in enumerate(halo_sides(halo_a_ref, halo_b_ref, c)):
            right_ref[c, side] = halo * edge_w[side]
    for side in range(2):
        tile = pl.ds(8 * side, 8)
        here = rows == 7 * side
        values = [None] * 3
        for k in range(nz):
            ratio = ratio_ref[k, tile, :]
            for c in range(3):
                value = jnp.where(here, right_ref[c, side, k : k + 1, :], 0.0)
                if k:
                    value = value + ratio * values[c]
                values[c] = value
                out_ref[c, k, tile, :] = value
        for k in range(nz - 1, -1, -1):
            recip = recip_ref[k, tile, :]
            for c in range(3):
                value = out_ref[c, k, tile, :] * recip
                if k < nz - 1:
                    value = value + ratio_ref[k + 1, tile, :] * values[c]
                values[c] = value
                out_ref[c, k, tile, :] = value + solved_ref[c, k, tile, :]


def own_pair(half, keep_ref, recv_ref, i):
    mine, other = keep_ref[i], recv_ref[i]
    return jnp.where(half == 0, mine, other), jnp.where(half == 0, other, mine)


def chip_coef_kernel(keep, recv, out_ref, mid_ref):
    half = lax.rem(lax.axis_index("gz"), 2)
    a0, a1 = own_pair(half, keep, recv, 0)
    c0, c1 = own_pair(half, keep, recv, 1)
    d0, d1 = own_pair(half, keep, recv, 2)
    inv = 1.0 / (d0 + a1)
    out_ref[0] = a0 - c0 * c0 * inv
    out_ref[1] = c0 * c1 * inv
    out_ref[2] = d1 - c1 * c1 * inv
    mid_ref[0] = inv
    mid_ref[1] = c0
    mid_ref[2] = c1


def join_coef_kernel(chips, *refs):
    own_ref, others, mask_ref = refs[0], refs[1:chips], refs[chips]
    below_ref, above_ref, own_out, all_ref = refs[chips + 1 :]
    index = lax.axis_index("gz")
    chip, half = lax.div(index, 2), lax.rem(index, 2)
    all_ref[chip] = own_ref[...]
    for j in range(1, chips):
        all_ref[chip ^ j] = others[j - 1][...]
    mask = mask_ref[...].astype(F32)
    mask = jnp.where(half == 0, mask[:8], mask[8:])
    zero = jnp.zeros(mask.shape, F32)

    low = zero
    for t in range(chips - 1):
        cross = all_ref[t, 1]
        kappa = cross / (all_ref[t, 0] + low)
        if t == 0:
            kappa = kappa * mask
        below_ref[t] = kappa
        low = jnp.where(t < chip, all_ref[t, 2] - kappa * cross, low)
    below_ref[chips - 1] = zero

    high = zero
    above_ref[chips - 1] = zero
    above_ref[0] = zero
    for t in range(chips - 1, 0, -1):
        cross = all_ref[t, 1]
        kappa = zero if t == chips - 1 else cross / (all_ref[t, 2] + high)
        above_ref[t] = kappa
        high = jnp.where(t > chip, all_ref[t, 0] - kappa * cross, high)

    near, cross, far = own_ref[0], own_ref[1], own_ref[2]
    bottom_on = jnp.where(chip == 0, mask, 1.0)
    top_on = jnp.where(chip == chips - 1, 0.0, 1.0)
    up = cross * bottom_on / (near + low)
    down = cross * top_on / (far + high)
    own_out[0] = up
    own_out[1] = down
    own_out[2] = bottom_on / (low + near - down * cross)
    own_out[3] = top_on / (high + far - up * cross)


def chip_values(half, keep, recv, mid_ref, volt_ref, c):
    inv, c0, c1 = mid_ref[0], mid_ref[1], mid_ref[2]
    first0, first1 = own_pair(half, keep, recv, c)
    last0, last1 = own_pair(half, keep, recv, 3 + c)
    current = (last0 - first1) * inv
    first = first0 - c0 * current
    last = last1 + c1 * current
    volt_ref[c] = first
    volt_ref[3 + c] = last
    volt_ref[6 + c] = current
    return first, last


def chip_kernel(keep, recv, mid_ref, volt_ref, own_ref):
    half = lax.rem(lax.axis_index("gz"), 2)
    for c in range(3):
        own_ref[c], own_ref[3 + c] = chip_values(half, keep, recv, mid_ref, volt_ref, c)


def chip_again_kernel(chips, keep, recv, mid_ref, own_coef, volt_ref, *parts):
    index = lax.axis_index("gz")
    chip, half = lax.div(index, 2), lax.rem(index, 2)
    up, down = own_coef[0], own_coef[1]
    for c in range(3):
        first, last = chip_values(half, keep, recv, mid_ref, volt_ref, c)
        to_above = last - up * first
        to_below = first - down * last
        for j in range(1, chips):
            parts[j - 1][c] = jnp.where((chip ^ j) > chip, to_above, to_below)


def join_kernel(chips, scaled, *refs):
    others = refs[: chips - 1]
    volt_ref, mid_ref, below_ref, above_ref, own_coef = refs[chips - 1 : chips + 4]
    keep_ref, send_ref, all_ref = refs[chips + 4 :]
    index = lax.axis_index("gz")
    chip, half = lax.div(index, 2), lax.rem(index, 2)
    for j in range(1, chips):
        all_ref[chip ^ j] = others[j - 1][...]
    all_ref[chip] = jnp.zeros(all_ref.shape[1:], F32)
    inv, c0, c1 = mid_ref[0], mid_ref[1], mid_ref[2]
    up, down, bottom_g, top_g = (own_coef[i] for i in range(4))
    for c in range(3):
        low = jnp.zeros(inv.shape, F32)
        for t in range(chips - 1):
            if scaled:
                value = all_ref[t, c] + below_ref[t] * low
            else:
                value = all_ref[t, 3 + c] + below_ref[t] * (low - all_ref[t, c])
            low = jnp.where(t < chip, value, low)
        high = jnp.zeros(inv.shape, F32)
        for t in range(chips - 1, 0, -1):
            if scaled:
                value = all_ref[t, c] + above_ref[t] * high
            else:
                value = all_ref[t, c] + above_ref[t] * (high - all_ref[t, 3 + c])
            high = jnp.where(t > chip, value, high)
        first, last = volt_ref[c], volt_ref[3 + c]
        j_bottom = (low - first - down * (high - last)) * bottom_g
        j_top = (last + up * (low - first) - high) * top_g
        j_mid = volt_ref[6 + c] + (c0 * j_bottom + c1 * j_top) * inv
        keep_ref[c] = jnp.where(half == 0, j_bottom, j_mid)
        keep_ref[3 + c] = jnp.where(half == 0, j_mid, j_top)
        send_ref[c] = jnp.where(half == 0, j_mid, j_bottom)
        send_ref[3 + c] = jnp.where(half == 0, j_top, j_mid)


def update_kernel(solved_ref, bottom_ref, top_ref, keep_ref, recv_ref, *outs):
    out_ref = outs[0]
    _, nz, nx, ny = solved_ref.shape
    half = lax.rem(lax.axis_index("gz"), 2)
    even = lax.rem(lax.axis_index("gx"), 2) == 0
    for c in range(3):
        j_bottom = jnp.concatenate(own_pair(half, keep_ref, recv_ref, c), 0)
        j_top = jnp.concatenate(own_pair(half, keep_ref, recv_ref, 3 + c), 0)
        for k in range(nz):
            value = solved_ref[c, k] + bottom_ref[k] * j_bottom - top_ref[k] * j_top
            out_ref[c, k] = value
            if len(outs) > 1:
                first, last = value[0:1], value[nx - 1 : nx]
                outs[1][c, k : k + 1, :] = jnp.where(even, last, first)
                outs[2][c, k : k + 1, :] = jnp.where(even, first, last)


def per_device(strips, slabs, adjoint, base_flow, conductance, ground_mask, turbine_cells, yaw_bin, yaw_table):
    _, nz, nx, ny = adjoint.shape
    chips = slabs // 2
    cube, field, plane = (nz, nx, ny), adjoint.shape, (3, nz, ny)
    pair_a = [(i, i ^ 1) for i in range(strips)]
    pair_b = [((i + 1) % strips, ((i ^ 1) + 1) % strips) for i in range(strips)]
    cores = [(i, i ^ 1) for i in range(slabs)]

    def across(parts):
        return [
            lax.ppermute(part, "gz", [(i, i ^ (2 * (j + 1))) for i in range(slabs)])
            for j, part in enumerate(parts)
        ]

    part = lambda n: (n, 8, ny)
    ratio, recip, bottom_w, top_w, keep, send = call(
        slab_kernel, [cube, cube, cube, cube, part(3), part(3)], (conductance,), 0.3
    )
    edge_a, edge_b = call(edge_kernel, [plane, plane], (adjoint,), 0.2, after=AFTER_EDGE(keep))
    recv = lax.ppermute(send, "gz", cores)
    own, mid = call(chip_coef_kernel, [part(3), part(3)], (keep, recv), 0.2)
    coefs = across([own] * (chips - 1))
    (source,) = call(
        source_kernel,
        [field],
        (turbine_cells, yaw_bin, yaw_table),
        3.5,
        [SMEM, SMEM, SMEM],
        after=AFTER_SOURCE(own),
    )
    state = adjoint
    for sweep_index in range(SWEEPS):
        halo_a = lax.ppermute(edge_a, "gx", pair_a)
        halo_b = lax.ppermute(edge_b, "gx", pair_b)
        first = sweep_index == 0
        extra = [(2, nz, ny), (2, 2, nz, ny)] if first else []
        solved, ends, *extra = call(
            right_kernel,
            [field, (6, nx, ny), *extra],
            (state, base_flow, source, ratio, recip, bottom_w, top_w),
            3.0,
        )
        if first:
            edge_w, end_w = extra
        keep, send = call(ends_kernel, [part(6), part(6)], (ends, halo_a, halo_b, end_w), 0.3)
        recv = lax.ppermute(send, "gz", cores)
        if first and not EARLY:
            volts, mine = call(chip_kernel, [part(9), part(6)], (keep, recv, mid), 0.2)
            others = across([mine] * (chips - 1))
        if first:
            below, above, own_coef = call(
                functools.partial(join_coef_kernel, chips),
                [(chips, 8, ny), (chips, 8, ny), part(4)],
                (own, *coefs, ground_mask),
                0.2,
                scratch=[pltpu.VMEM((chips, 3, 8, ny), F32)],
            )
        if not first or EARLY:
            volts, *parts = call(
                functools.partial(chip_again_kernel, chips),
                [part(9)] + [part(3)] * (chips - 1),
                (keep, recv, mid, own_coef),
                0.2,
            )
            others = across(parts)
        (solved,) = call(
            halo_kernel,
            [field],
            (solved, halo_a, halo_b, edge_w, ratio, recip),
            1.0,
            scratch=[pltpu.VMEM((3, 2, nz, ny), F32)],
        )
        scaled = not first or EARLY
        j_keep, j_send = call(
            functools.partial(join_kernel, chips, scaled),
            [part(6), part(6)],
            (*others, volts, mid, below, above, own_coef),
            0.2,
            scratch=[pltpu.VMEM((chips, 3 if scaled else 6, 8, ny), F32)],
        )
        j_recv = lax.ppermute(j_send, "gz", cores)
        last = sweep_index == SWEEPS - 1
        edges = [] if last else [plane] * 2
        state, *edges = call(
            update_kernel, [field, *edges], (solved, bottom_w, top_w, j_keep, j_recv), 0.5
        )
        if not last:
            edge_a, edge_b = edges
    return state


def solution(mesh):
    in_specs = (
        P(None, "gz", "gx", None),
        P(None, "gz", "gx", None),
        P("gz", "gx", None),
        P("gx", None),
        P(),
        P(),
        P(),
    )
    out_specs = P(None, "gz", "gx", None)
    body = functools.partial(per_device, mesh.shape["gx"], mesh.shape["gz"])
    return jax.shard_map(body, mesh=mesh, in_specs=in_specs, out_specs=out_specs, check_vma=False)
```

```python
import functools

import jax
import jax.numpy as jnp
from jax import lax
from jax.experimental import pallas as pl
from jax.experimental.pallas import tpu as pltpu
from jax.sharding import PartitionSpec as P

SWEEPS = 2
PSEUDO_STEP = 0.2
LATERAL_VISC = 1.0


F32 = jnp.float32
VMEM = pl.BlockSpec(memory_space=pltpu.VMEM)
SMEM = pl.BlockSpec(memory_space=pltpu.SMEM)
ANY = pl.BlockSpec(memory_space=pl.ANY)
PARAMS = pltpu.CompilerParams(vmem_limit_bytes=12 * 1024 * 1024)


def call(body, outs, ins, cost_us, specs=None, scratch=(), after=()):
    def run(*refs):
        body(*refs[: len(ins)], *refs[len(ins) + len(after) :])

    return pl.pallas_call(
        run,
        out_shape=[jax.ShapeDtypeStruct(s, F32) for s in outs],
        in_specs=(specs or [VMEM] * len(ins)) + [ANY] * len(after),
        out_specs=[VMEM] * len(outs),
        scratch_shapes=list(scratch),
        compiler_params=PARAMS,
        cost_estimate=pl.CostEstimate(
            flops=0, bytes_accessed=int(cost_us * 3.0e6), transcendentals=0
        ),
    )(*ins, *after)


def chip_and_core():
    index = lax.axis_index("gz")
    return lax.div(index, 2), lax.rem(index, 2)


def share_kernel(whole_ref, keep_ref, send_ref, *inner_refs):
    parts, nz, nx, _ = whole_ref.shape
    half = nx // 2
    _, core = chip_and_core()
    mine = pl.ds(pl.multiple_of(core * half, half), half)
    other = pl.ds(pl.multiple_of((1 - core) * half, half), half)
    for c in range(parts):
        for k in range(nz):
            keep_ref[c, k] = whole_ref[c, k, mine, :]
            send_ref[c, k] = whole_ref[c, k, other, :]
            if inner_refs:
                before = whole_ref[c, k, half - 1 : half, :]
                behind = whole_ref[c, k, half : half + 1, :]
                at = nz + k // half, slice(k % half, k % half + 1)
                inner_refs[0][c, k : k + 1, :] = jnp.where(core == 0, behind, before)
                send_ref[c, at[0], at[1], :] = jnp.where(core == 0, before, behind)


def store_edges(core, c, k, first, last, outer_ref, inner_ref):
    outer_ref[c, k : k + 1, :] = jnp.where(core == 0, first, last)
    inner_ref[c, k : k + 1, :] = jnp.where(core == 0, last, first)


def gather_kernel(keep_ref, recv_ref, out_ref):
    parts, nz, _, _ = keep_ref.shape
    _, core = chip_and_core()
    for c in range(parts):
        for k in range(nz):
            out_ref[c, core * nz + k] = keep_ref[c, k]
            out_ref[c, (1 - core) * nz + k] = recv_ref[c, k]


def gather_state_kernel(keep_ref, recv_ref, row_ref, out_ref, outer_ref, inner_ref):
    parts, nz, nx, _ = keep_ref.shape
    gather_kernel(keep_ref, recv_ref, out_ref)
    _, core = chip_and_core()
    for c in range(parts):
        inner_ref[c, pl.ds(pl.multiple_of(core * nz, nz), nz), :] = row_ref[c]
        for i in range(nz // nx):
            at = pl.ds(pl.multiple_of((1 - core) * nz + i * nx, nx), nx)
            inner_ref[c, at, :] = recv_ref[c, nz + i]
        for k in range(2 * nz):
            first, last = out_ref[c, k, 0:1, :], out_ref[c, k, nx - 1 : nx, :]
            outer_ref[c, k : k + 1, :] = jnp.where(core == 0, first, last)


def source_kernel(cells_ref, bin_ref, table_ref, source_ref):
    parts, nz, nx, ny = source_ref.shape
    count = cells_ref.shape[1]
    chip, core = chip_and_core()
    lz = cells_ref[0:1, :] - chip * nz
    lx = cells_ref[1:2, :] - (lax.axis_index("gx") * 2 + core) * nx
    inside = (lz >= 0) & (lz < nz) & (lx >= 0) & (lx < nx)
    row = jnp.where(inside, lz * nx + lx, -1)
    at_row = lax.broadcasted_iota(jnp.int32, (nz * nx, count), 0) == row
    at_lane = lax.broadcasted_iota(jnp.int32, (ny, count), 0) == cells_ref[2:3, :]
    at_lane = jnp.where(at_lane, 1.0, 0.0)
    bins = [bin_ref[...] == b for b in range(table_ref.shape[1])]
    for c in range(parts):
        strength = jnp.zeros((1, count), F32)
        for b, here in enumerate(bins):
            strength = jnp.where(here, table_ref[c : c + 1, b : b + 1], strength)
        placed = lax.dot_general(
            jnp.where(at_row, strength, 0.0),
            at_lane,
            (((1,), (1,)), ((), ())),
            precision=lax.Precision.HIGHEST,
            preferred_element_type=F32,
        )
        source_ref[c] = placed.reshape(nz, nx, ny)


def slab_kernel(keep_ref, recv_ref, ratio_ref, recip_ref, bottom_ref, top_ref, own_ref, w_ref, cond_ref):
    nz, nx, ny = cond_ref.shape
    half = nz // 2
    _, core = chip_and_core()
    for k in range(half):
        cond_ref[core * half + k] = keep_ref[0, k]
        cond_ref[(1 - core) * half + k] = recv_ref[0, k]
    sigma = jnp.ones((nx, ny), F32)
    tau = jnp.ones((nx, ny), F32)
    for k in range(nz - 1):
        face = cond_ref[k + 1]
        recip = 1.0 / (sigma + face)
        ratio = face * recip
        recip_ref[k] = recip
        ratio_ref[k + 1] = ratio
        sigma = 1.0 + sigma * ratio
        face = cond_ref[nz - 1 - k]
        ratio = face / (tau + face)
        bottom_ref[nz - 1 - k] = ratio
        tau = 1.0 + tau * ratio
    weight = 1.0 / sigma
    recip_ref[nz - 1] = weight
    ratio_ref[0] = jnp.zeros((nx, ny), F32)
    own_ref[2] = weight
    top_ref[nz - 1] = weight
    for k in range(nz - 2, -1, -1):
        weight = weight * ratio_ref[k + 1]
        top_ref[k] = weight
    own_ref[1] = weight
    weight = 1.0 / tau
    own_ref[0] = weight + 1.0 / cond_ref[0]
    bottom_ref[0] = weight
    for k in range(1, nz):
        weight = weight * bottom_ref[k]
        bottom_ref[k] = weight
    for k in range(half):
        w_ref[0, k] = bottom_ref[(1 - core) * half + k]
        w_ref[1, k] = top_ref[(1 - core) * half + k]


def right_kernel(
    state_ref, flow_ref, source_ref, ratio_ref, recip_ref, bottom_ref, top_ref,
    solved_ref, ends_ref, *edge_refs,
):
    _, nz, nx, ny = state_ref.shape
    lanes = lax.broadcasted_iota(jnp.int32, (nx, ny), 1)
    rows = lax.broadcasted_iota(jnp.int32, (nx, ny), 0)
    visc = PSEUDO_STEP * LATERAL_VISC
    values = [None] * 3
    for k in range(nz):
        u = 0.5 * PSEUDO_STEP * flow_ref[0, k]
        v = 0.5 * PSEUDO_STEP * flow_ref[1, k]
        x_plus_w = visc + u
        x_minus_w = visc - u
        if edge_refs:
            edge_w, end_w = edge_refs
            for side, weight in ((0, x_minus_w[0:1]), (1, x_plus_w[nx - 1 : nx])):
                row = pl.ds(side * (nx - 1), 1)
                edge_w[side, k : k + 1, :] = weight
                end_w[side, 0, k : k + 1, :] = weight * bottom_ref[k, row, :]
                end_w[side, 1, k : k + 1, :] = weight * top_ref[k, row, :]
        x_plus_w = jnp.where(rows == nx - 1, 0.0, x_plus_w)
        x_minus_w = jnp.where(rows == 0, 0.0, x_minus_w)
        y_plus_w = jnp.where(lanes == ny - 1, 0.0, visc + v)
        y_minus_w = jnp.where(lanes == 0, 0.0, visc - v)
        ratio = ratio_ref[k]
        for c in range(3):
            a = state_ref[c, k]
            value = (
                (1.0 - 4.0 * visc) * a
                + x_plus_w * pltpu.roll(a, nx - 1, 0)
                + x_minus_w * pltpu.roll(a, 1, 0)
                + y_plus_w * pltpu.roll(a, ny - 1, 1)
                + y_minus_w * pltpu.roll(a, 1, 1)
                + source_ref[c, k]
            )
            if k:
                value = value + ratio * values[c]
            values[c] = value
            solved_ref[c, k] = value
    for k in range(nz - 1, -1, -1):
        recip = recip_ref[k]
        for c in range(3):
            value = solved_ref[c, k] * recip
            if k < nz - 1:
                value = value + ratio_ref[k + 1] * values[c]
            else:
                ends_ref[3 + c] = value
            values[c] = value
            solved_ref[c, k] = value
    for c in range(3):
        ends_ref[c] = values[c]


def halo_sides(outer_ref, inner_ref, c):
    _, core = chip_and_core()
    strip = lax.axis_index("gx")
    wall = jnp.where(core == 0, strip == 0, strip == lax.axis_size("gx") - 1)
    outer = outer_ref[c] * jnp.where(wall, 0.0, 1.0)
    inner = inner_ref[c]
    return jnp.where(core == 0, outer, inner), jnp.where(core == 0, inner, outer)


def ends_kernel(chips, ends_ref, outer_ref, inner_ref, end_w, own_coef, volt_ref, *parts):
    chip, _ = chip_and_core()
    nx = ends_ref.shape[1]
    rows = lax.broadcasted_iota(jnp.int32, ends_ref.shape[1:], 0)
    up, down = own_coef[0], own_coef[1]
    for c in range(3):
        left, right = halo_sides(outer_ref, inner_ref, c)
        both = []
        for e in range(2):
            low = jnp.sum(left * end_w[0, e], 0, keepdims=True)
            high = jnp.sum(right * end_w[1, e], 0, keepdims=True)
            value = ends_ref[3 * e + c] + jnp.where(rows == 0, low, 0.0)
            value = value + jnp.where(rows == nx - 1, high, 0.0)
            volt_ref[3 * e + c] = value
            both.append(value)
        first, last = both
        to_above = last - up * first
        to_below = first - down * last
        for j in range(1, chips):
            parts[j - 1][c] = jnp.where((chip ^ j) > chip, to_above, to_below)


def halo_kernel(solved_ref, outer_ref, inner_ref, edge_w, ratio_ref, recip_ref, out_ref, *refs):
    _, nz, nx, ny = solved_ref.shape
    right_ref = refs[-1]
    rows = lax.broadcasted_iota(jnp.int32, (nx, ny), 0)
    for c in range(3):
        for side, halo in enumerate(halo_sides(outer_ref, inner_ref, c)):
            right_ref[c, side] = halo * edge_w[side]
    values = [None] * 3
    for k in range(nz):
        ratio = ratio_ref[k]
        for c in range(3):
            value = jnp.where(rows == 0, right_ref[c, 0, k : k + 1, :], 0.0)
            value = jnp.where(rows == nx - 1, right_ref[c, 1, k : k + 1, :], value)
            if k:
                value = value + ratio * values[c]
            values[c] = value
            out_ref[c, k] = value
    for k in range(nz - 1, -1, -1):
        recip = recip_ref[k]
        for c in range(3):
            value = out_ref[c, k] * recip
            if k < nz - 1:
                value = value + ratio_ref[k + 1] * values[c]
            values[c] = value
            out_ref[c, k] = value + solved_ref[c, k]
    if len(refs) > 1:
        half = nz // 2
        _, core = chip_and_core()
        for c in range(3):
            for k in range(half):
                refs[0][c, k] = out_ref[c, (1 - core) * half + k]


def join_coef_kernel(chips, *refs):
    own_ref, others, mask_ref = refs[0], refs[1:chips], refs[chips]
    below_ref, above_ref, own_out, all_ref = refs[chips + 1 :]
    chip, core = chip_and_core()
    nx = own_ref.shape[1]
    all_ref[chip] = own_ref[...]
    for j in range(1, chips):
        all_ref[chip ^ j] = others[j - 1][...]
    mask = mask_ref[pl.ds(pl.multiple_of(core * nx, nx), nx), :].astype(F32)
    zero = jnp.zeros(mask.shape, F32)

    low = zero
    for t in range(chips - 1):
        cross = all_ref[t, 1]
        kappa = cross / (all_ref[t, 0] + low)
        if t == 0:
            kappa = kappa * mask
        below_ref[t] = kappa
        low = jnp.where(t < chip, all_ref[t, 2] - kappa * cross, low)
    below_ref[chips - 1] = zero

    high = zero
    above_ref[chips - 1] = zero
    above_ref[0] = zero
    for t in range(chips - 1, 0, -1):
        cross = all_ref[t, 1]
        kappa = zero if t == chips - 1 else cross / (all_ref[t, 2] + high)
        above_ref[t] = kappa
        high = jnp.where(t > chip, all_ref[t, 0] - kappa * cross, high)

    near, cross, far = own_ref[0], own_ref[1], own_ref[2]
    bottom_on = jnp.where(chip == 0, mask, 1.0)
    top_on = jnp.where(chip == chips - 1, 0.0, 1.0)
    up = cross * bottom_on / (near + low)
    down = cross * top_on / (far + high)
    own_out[0] = up
    own_out[1] = down
    own_out[2] = bottom_on / (low + near - down * cross)
    own_out[3] = top_on / (high + far - up * cross)


def join_kernel(chips, whole, *refs):
    others = refs[: chips - 1]
    volt_ref, below_ref, above_ref, own_coef = refs[chips - 1 : chips + 3]
    rest, all_ref = refs[chips + 3 : -1], refs[-1]
    chip, core = chip_and_core()
    for j in range(1, chips):
        all_ref[chip ^ j] = others[j - 1][...]
    all_ref[chip] = jnp.zeros(all_ref.shape[1:], F32)
    up, down, bottom_g, top_g = (own_coef[i] for i in range(4))
    for c in range(3):
        low = jnp.zeros(up.shape, F32)
        for t in range(chips - 1):
            low = jnp.where(t < chip, all_ref[t, c] + below_ref[t] * low, low)
        high = jnp.zeros(up.shape, F32)
        for t in range(chips - 1, 0, -1):
            high = jnp.where(t > chip, all_ref[t, c] + above_ref[t] * high, high)
        first, last = volt_ref[c], volt_ref[3 + c]
        j_bottom = (low - first - down * (high - last)) * bottom_g
        j_top = (last + up * (low - first) - high) * top_g
        if not whole:
            rest[0][c] = j_bottom
            rest[0][3 + c] = j_top
            continue
        solved_ref, bottom_ref, top_ref, out_ref, outer_ref, inner_ref = rest
        nz, nx, _ = bottom_ref.shape
        for k in range(nz):
            value = solved_ref[c, k] + bottom_ref[k] * j_bottom - top_ref[k] * j_top
            out_ref[c, k] = value
            store_edges(core, c, k, value[0:1], value[nx - 1 : nx], outer_ref, inner_ref)


def last_kernel(
    solved_ref, bottom_ref, top_ref, j_ref, solved_other, w_other, j_other, out_ref
):
    half = solved_other.shape[1]
    nx = solved_ref.shape[2]
    _, core = chip_and_core()
    mine = pl.ds(pl.multiple_of(core * nx, nx), nx)
    other = pl.ds(pl.multiple_of((1 - core) * nx, nx), nx)
    for c in range(3):
        for k in range(half):
            at = core * half + k
            out_ref[c, k, mine, :] = (
                solved_ref[c, at] + bottom_ref[at] * j_ref[c] - top_ref[at] * j_ref[3 + c]
            )
            out_ref[c, k, other, :] = (
                solved_other[c, k] + w_other[0, k] * j_other[c] - w_other[1, k] * j_other[3 + c]
            )


def per_device(strips, slabs, adjoint, base_flow, conductance, ground_mask, turbine_cells, yaw_bin, yaw_table):
    _, nz, nx, ny = adjoint.shape
    half, chips, levels = nx // 2, slabs // 2, 2 * nz
    cube, field, plane = (levels, half, ny), (3, levels, half, ny), (3, levels, ny)
    cores = [(i, i ^ 1) for i in range(slabs)]
    facing = []
    for strip in range(strips):
        for slab in range(slabs):
            other = strip + (1 if slab % 2 else -1)
            there = other * slabs + (slab ^ 1) if 0 <= other < strips else strip * slabs + (slab ^ 2)
            facing.append((strip * slabs + slab, there))

    def swap(part):
        return lax.ppermute(part, "gz", cores)

    def face(outer):
        return lax.ppermute(outer, ("gx", "gz"), facing)

    def across(parts):
        return [
            lax.ppermute(part, "gz", [(i, i ^ (2 * (j + 1))) for i in range(slabs)])
            for j, part in enumerate(parts)
        ]

    def share(whole, after=()):
        shape = (whole.shape[0], nz, half, ny)
        keep, send = call(share_kernel, [shape, shape], (whole,), 0.3, after=after)
        return keep, swap(send)

    part = lambda n: (n, half, ny)
    keep, recv = share(conductance[None])
    ratio, recip, bottom_w, top_w, own, w_send = call(
        slab_kernel,
        [cube, cube, cube, cube, part(3), (2, nz, half, ny)],
        (keep, recv),
        0.5,
        scratch=[pltpu.VMEM(cube, F32)],
    )
    coefs = across([own] * (chips - 1))
    extra = -(-nz // half)
    keep, send, row = call(
        share_kernel,
        [(3, nz, half, ny), (3, nz + extra, half, ny), (3, nz, ny)],
        (adjoint,),
        0.3,
        after=[recv],
    )
    flow_parts = share(base_flow, [keep])
    state, outer, inner = call(
        gather_state_kernel, [field, plane, plane], (keep, swap(send), row), 0.5, after=[own]
    )
    (flow,) = call(gather_kernel, [(2, *cube)], flow_parts, 0.3)
    (source,) = call(
        source_kernel, [field], (turbine_cells, yaw_bin[None], yaw_table), 1.0, after=[own]
    )
    for sweep_index in range(SWEEPS):
        first, last = sweep_index == 0, sweep_index == SWEEPS - 1
        outer = face(outer)
        if not first:
            inner = swap(inner)
        extra = [(2, levels, ny), (2, 2, levels, ny)] if first else []
        solved, ends, *extra = call(
            right_kernel,
            [field, part(6), *extra],
            (state, flow, source, ratio, recip, bottom_w, top_w),
            1.5,
        )
        if first:
            edge_w, end_w = extra
            below, above, own_coef = call(
                functools.partial(join_coef_kernel, chips),
                [(chips, half, ny), (chips, half, ny), part(4)],
                (own, *coefs, ground_mask),
                0.1,
                after=[ends],
                scratch=[pltpu.VMEM((chips, 3, half, ny), F32)],
            )
        volts, *parts = call(
            functools.partial(ends_kernel, chips),
            [part(6)] + [part(3)] * (chips - 1),
            (ends, outer, inner, end_w, own_coef),
            0.2,
        )
        others = across(parts)
        solved, *send = call(
            halo_kernel,
            [field] + ([(3, nz, half, ny)] if last else []),
            (solved, outer, inner, edge_w, ratio, recip),
            0.4,
            scratch=[pltpu.VMEM((3, 2, levels, ny), F32)],
        )
        more = () if last else (solved, bottom_w, top_w)
        outs = call(
            functools.partial(join_kernel, chips, not last),
            [part(6)] if last else [field, plane, plane],
            (*others, volts, below, above, own_coef, *more),
            0.4,
            scratch=[pltpu.VMEM((chips, 3, half, ny), F32)],
        )
        if not last:
            state, outer, inner = outs
    solved_other, w_other = swap(send[0]), swap(w_send)
    (currents,) = outs
    (out,) = call(
        last_kernel,
        [adjoint.shape],
        (solved, bottom_w, top_w, currents, solved_other, w_other, swap(currents)),
        1.0,
    )
    return out


def solution(mesh):
    in_specs = (
        P(None, "gz", "gx", None),
        P(None, "gz", "gx", None),
        P("gz", "gx", None),
        P("gx", None),
        P(),
        P(),
        P(),
    )
    out_specs = P(None, "gz", "gx", None)
    body = functools.partial(per_device, mesh.shape["gx"], mesh.shape["gz"])
    return jax.shard_map(body, mesh=mesh, in_specs=in_specs, out_specs=out_specs, check_vma=False)
```

```python
import functools

import jax
import jax.numpy as jnp
from jax import lax
from jax.experimental import pallas as pl
from jax.experimental.pallas import tpu as pltpu
from jax.sharding import PartitionSpec as P

SWEEPS = 2
PSEUDO_STEP = 0.2
LATERAL_VISC = 1.0


F32 = jnp.float32
VMEM = pl.BlockSpec(memory_space=pltpu.VMEM)
ANY = pl.BlockSpec(memory_space=pl.ANY)


def call(body, outs, ins, cost_us, specs=None, scratch=(), after=(), through=()):
    n, m, k = len(ins), len(ins) + len(after) + len(through), len(through)

    def run(*refs):
        body(*refs[:n], *refs[m : m + len(outs)], *refs[m + len(outs) + k :])

    return pl.pallas_call(
        run,
        out_shape=[jax.ShapeDtypeStruct(s, F32) for s in outs]
        + [jax.ShapeDtypeStruct(t.shape, F32) for t in through],
        in_specs=(specs or [VMEM] * n) + [ANY] * (m - n),
        out_specs=[VMEM] * len(outs) + [ANY] * k,
        input_output_aliases={m - k + i: len(outs) + i for i in range(k)},
        scratch_shapes=list(scratch),
        compiler_params=pltpu.CompilerParams(vmem_limit_bytes=12 * 1024 * 1024),
        cost_estimate=pl.CostEstimate(
            flops=0, bytes_accessed=int(cost_us * 3.0e6), transcendentals=0
        ),
    )(*ins, *after, *through)


def chip_and_core():
    index = lax.axis_index("gz")
    return lax.div(index, 2), lax.rem(index, 2)


def share_kernel(whole_ref, keep_ref, send_ref, *inner_refs):
    parts, nz, nx, _ = whole_ref.shape
    half = nx // 2
    _, core = chip_and_core()
    mine = pl.ds(pl.multiple_of(core * half, half), half)
    other = pl.ds(pl.multiple_of((1 - core) * half, half), half)
    for c in range(parts):
        for k in range(nz):
            keep_ref[c, k] = whole_ref[c, k, mine, :]
            send_ref[c, k] = whole_ref[c, k, other, :]
            if inner_refs:
                before = whole_ref[c, k, half - 1 : half, :]
                behind = whole_ref[c, k, half : half + 1, :]
                at = nz + k // half, slice(k % half, k % half + 1)
                inner_refs[0][c, k : k + 1, :] = jnp.where(core == 0, behind, before)
                send_ref[c, at[0], at[1], :] = jnp.where(core == 0, before, behind)


def store_edges(core, c, k, first, last, outer_ref, inner_ref):
    outer_ref[c, k : k + 1, :] = jnp.where(core == 0, first, last)
    inner_ref[c, k : k + 1, :] = jnp.where(core == 0, last, first)


def gather_kernel(keep_ref, recv_ref, out_ref):
    parts, nz, _, _ = keep_ref.shape
    _, core = chip_and_core()
    for c in range(parts):
        for k in range(nz):
            out_ref[c, core * nz + k] = keep_ref[c, k]
            out_ref[c, (1 - core) * nz + k] = recv_ref[c, k]


def gather_state_kernel(keep_ref, recv_ref, row_ref, out_ref, outer_ref, inner_ref):
    parts, nz, nx, _ = keep_ref.shape
    gather_kernel(keep_ref, recv_ref, out_ref)
    _, core = chip_and_core()
    for c in range(parts):
        inner_ref[c, pl.ds(pl.multiple_of(core * nz, nz), nz), :] = row_ref[c]
        for i in range(nz // nx):
            at = pl.ds(pl.multiple_of((1 - core) * nz + i * nx, nx), nx)
            inner_ref[c, at, :] = recv_ref[c, nz + i]
        for k in range(2 * nz):
            first, last = out_ref[c, k, 0:1, :], out_ref[c, k, nx - 1 : nx, :]
            outer_ref[c, k : k + 1, :] = jnp.where(core == 0, first, last)


def source_kernel(cells_ref, bin_ref, table_ref, source_ref):
    parts, nz, nx, ny = source_ref.shape
    count = cells_ref.shape[1]
    chip, core = chip_and_core()
    lz = cells_ref[0:1, :] - chip * nz
    lx = cells_ref[1:2, :] - (lax.axis_index("gx") * 2 + core) * nx
    inside = (lz >= 0) & (lz < nz) & (lx >= 0) & (lx < nx)
    row = jnp.where(inside, lz * nx + lx, -1)
    at_row = lax.broadcasted_iota(jnp.int32, (nz * nx, count), 0) == row
    at_lane = lax.broadcasted_iota(jnp.int32, (ny, count), 0) == cells_ref[2:3, :]
    at_lane = jnp.where(at_lane, 1.0, 0.0)
    bins = [bin_ref[...] == b for b in range(table_ref.shape[1])]
    for c in range(parts):
        strength = jnp.zeros((1, count), F32)
        for b, here in enumerate(bins):
            strength = jnp.where(here, table_ref[c : c + 1, b : b + 1], strength)
        placed = lax.dot_general(
            jnp.where(at_row, strength, 0.0),
            at_lane,
            (((1,), (1,)), ((), ())),
            precision=lax.Precision.HIGHEST,
            preferred_element_type=F32,
        )
        source_ref[c] = placed.reshape(nz, nx, ny)


def slab_kernel(keep_ref, recv_ref, ratio_ref, recip_ref, bottom_ref, top_ref, own_ref, w_ref, cond_ref):
    nz, nx, ny = cond_ref.shape
    half = nz // 2
    _, core = chip_and_core()
    for k in range(half):
        cond_ref[core * half + k] = keep_ref[0, k]
        cond_ref[(1 - core) * half + k] = recv_ref[0, k]
    sigma = jnp.ones((nx, ny), F32)
    tau = jnp.ones((nx, ny), F32)
    for k in range(nz - 1):
        face = cond_ref[k + 1]
        recip = 1.0 / (sigma + face)
        ratio = face * recip
        recip_ref[k] = recip
        ratio_ref[k + 1] = ratio
        sigma = 1.0 + sigma * ratio
        face = cond_ref[nz - 1 - k]
        ratio = face / (tau + face)
        bottom_ref[nz - 1 - k] = ratio
        tau = 1.0 + tau * ratio
    weight = 1.0 / sigma
    recip_ref[nz - 1] = weight
    ratio_ref[0] = jnp.zeros((nx, ny), F32)
    own_ref[2] = weight
    top_ref[nz - 1] = weight
    for k in range(nz - 2, -1, -1):
        weight = weight * ratio_ref[k + 1]
        top_ref[k] = weight
    own_ref[1] = weight
    weight = 1.0 / tau
    own_ref[0] = weight + 1.0 / cond_ref[0]
    bottom_ref[0] = weight
    for k in range(1, nz):
        weight = weight * bottom_ref[k]
        bottom_ref[k] = weight
    for k in range(half):
        w_ref[0, k] = bottom_ref[(1 - core) * half + k]
        w_ref[1, k] = top_ref[(1 - core) * half + k]


def right_kernel(
    state_ref, flow_ref, source_ref, ratio_ref, recip_ref, bottom_ref, top_ref,
    solved_ref, ends_ref, *edge_refs,
):
    _, nz, nx, ny = state_ref.shape
    lanes = lax.broadcasted_iota(jnp.int32, (nx, ny), 1)
    rows = lax.broadcasted_iota(jnp.int32, (nx, ny), 0)
    visc = PSEUDO_STEP * LATERAL_VISC
    values = [None] * 3
    for k in range(nz):
        u = 0.5 * PSEUDO_STEP * flow_ref[0, k]
        v = 0.5 * PSEUDO_STEP * flow_ref[1, k]
        x_plus_w = visc + u
        x_minus_w = visc - u
        if edge_refs:
            edge_w, end_w = edge_refs
            for side, weight in ((0, x_minus_w[0:1]), (1, x_plus_w[nx - 1 : nx])):
                row = pl.ds(side * (nx - 1), 1)
                edge_w[side, k : k + 1, :] = weight
                end_w[side, 0, k : k + 1, :] = weight * bottom_ref[k, row, :]
                end_w[side, 1, k : k + 1, :] = weight * top_ref[k, row, :]
        x_plus_w = jnp.where(rows == nx - 1, 0.0, x_plus_w)
        x_minus_w = jnp.where(rows == 0, 0.0, x_minus_w)
        y_plus_w = jnp.where(lanes == ny - 1, 0.0, visc + v)
        y_minus_w = jnp.where(lanes == 0, 0.0, visc - v)
        ratio = ratio_ref[k]
        for c in range(3):
            a = state_ref[c, k]
            value = (
                (1.0 - 4.0 * visc) * a
                + x_plus_w * pltpu.roll(a, nx - 1, 0)
                + x_minus_w * pltpu.roll(a, 1, 0)
                + y_plus_w * pltpu.roll(a, ny - 1, 1)
                + y_minus_w * pltpu.roll(a, 1, 1)
                + source_ref[c, k]
            )
            if k:
                value = value + ratio * values[c]
            values[c] = value
            solved_ref[c, k] = value
    for k in range(nz - 1, -1, -1):
        recip = recip_ref[k]
        for c in range(3):
            value = solved_ref[c, k] * recip
            if k < nz - 1:
                value = value + ratio_ref[k + 1] * values[c]
            else:
                ends_ref[3 + c] = value
            values[c] = value
            solved_ref[c, k] = value
    for c in range(3):
        ends_ref[c] = values[c]


def halo_sides(outer_ref, inner_ref, c):
    _, core = chip_and_core()
    strip = lax.axis_index("gx")
    wall = jnp.where(core == 0, strip == 0, strip == lax.axis_size("gx") - 1)
    outer = outer_ref[c] * jnp.where(wall, 0.0, 1.0)
    inner = inner_ref[c]
    return jnp.where(core == 0, outer, inner), jnp.where(core == 0, inner, outer)


def ends_kernel(chips, ends_ref, outer_ref, inner_ref, end_w, own_coef, volt_ref, *parts):
    chip, _ = chip_and_core()
    nx = ends_ref.shape[1]
    rows = lax.broadcasted_iota(jnp.int32, ends_ref.shape[1:], 0)
    up, down = own_coef[0], own_coef[1]
    for c in range(3):
        left, right = halo_sides(outer_ref, inner_ref, c)
        both = []
        for e in range(2):
            low = jnp.sum(left * end_w[0, e], 0, keepdims=True)
            high = jnp.sum(right * end_w[1, e], 0, keepdims=True)
            value = ends_ref[3 * e + c] + jnp.where(rows == 0, low, 0.0)
            value = value + jnp.where(rows == nx - 1, high, 0.0)
            volt_ref[3 * e + c] = value
            both.append(value)
        first, last = both
        to_above = last - up * first
        to_below = first - down * last
        for j in range(1, chips):
            parts[j - 1][c] = jnp.where((chip ^ j) > chip, to_above, to_below)


def halo_kernel(solved_ref, outer_ref, inner_ref, edge_w, ratio_ref, recip_ref, out_ref, *refs):
    _, nz, nx, ny = solved_ref.shape
    right_ref = refs[-1]
    rows = lax.broadcasted_iota(jnp.int32, (nx, ny), 0)
    for c in range(3):
        for side, halo in enumerate(halo_sides(outer_ref, inner_ref, c)):
            right_ref[c, side] = halo * edge_w[side]
    values = [None] * 3
    for k in range(nz):
        ratio = ratio_ref[k]
        for c in range(3):
            value = jnp.where(rows == 0, right_ref[c, 0, k : k + 1, :], 0.0)
            value = jnp.where(rows == nx - 1, right_ref[c, 1, k : k + 1, :], value)
            if k:
                value = value + ratio * values[c]
            values[c] = value
            out_ref[c, k] = value
    for k in range(nz - 1, -1, -1):
        recip = recip_ref[k]
        for c in range(3):
            value = out_ref[c, k] * recip
            if k < nz - 1:
                value = value + ratio_ref[k + 1] * values[c]
            values[c] = value
            out_ref[c, k] = value + solved_ref[c, k]
    if len(refs) > 1:
        half = nz // 2
        _, core = chip_and_core()
        for c in range(3):
            for k in range(half):
                refs[0][c, k] = out_ref[c, (1 - core) * half + k]


def join_coef_kernel(chips, *refs):
    own_ref, others, mask_ref = refs[0], refs[1:chips], refs[chips]
    below_ref, above_ref, own_out, all_ref = refs[chips + 1 :]
    chip, core = chip_and_core()
    nx = own_ref.shape[1]
    all_ref[chip] = own_ref[...]
    for j in range(1, chips):
        all_ref[chip ^ j] = others[j - 1][...]
    mask = mask_ref[pl.ds(pl.multiple_of(core * nx, nx), nx), :].astype(F32)
    zero = jnp.zeros(mask.shape, F32)

    low = zero
    for t in range(chips - 1):
        cross = all_ref[t, 1]
        kappa = cross / (all_ref[t, 0] + low)
        if t == 0:
            kappa = kappa * mask
        below_ref[t] = kappa
        low = jnp.where(t < chip, all_ref[t, 2] - kappa * cross, low)
    below_ref[chips - 1] = zero

    high = zero
    above_ref[chips - 1] = zero
    above_ref[0] = zero
    for t in range(chips - 1, 0, -1):
        cross = all_ref[t, 1]
        kappa = zero if t == chips - 1 else cross / (all_ref[t, 2] + high)
        above_ref[t] = kappa
        high = jnp.where(t > chip, all_ref[t, 0] - kappa * cross, high)

    near, cross, far = own_ref[0], own_ref[1], own_ref[2]
    bottom_on = jnp.where(chip == 0, mask, 1.0)
    top_on = jnp.where(chip == chips - 1, 0.0, 1.0)
    up = cross * bottom_on / (near + low)
    down = cross * top_on / (far + high)
    own_out[0] = up
    own_out[1] = down
    own_out[2] = bottom_on / (low + near - down * cross)
    own_out[3] = top_on / (high + far - up * cross)


def join_kernel(chips, whole, *refs):
    others = refs[: chips - 1]
    volt_ref, below_ref, above_ref, own_coef = refs[chips - 1 : chips + 3]
    rest, all_ref = refs[chips + 3 : -1], refs[-1]
    chip, core = chip_and_core()
    for j in range(1, chips):
        all_ref[chip ^ j] = others[j - 1][...]
    all_ref[chip] = jnp.zeros(all_ref.shape[1:], F32)
    up, down, bottom_g, top_g = (own_coef[i] for i in range(4))
    for c in range(3):
        low = jnp.zeros(up.shape, F32)
        for t in range(chips - 1):
            low = jnp.where(t < chip, all_ref[t, c] + below_ref[t] * low, low)
        high = jnp.zeros(up.shape, F32)
        for t in range(chips - 1, 0, -1):
            high = jnp.where(t > chip, all_ref[t, c] + above_ref[t] * high, high)
        first, last = volt_ref[c], volt_ref[3 + c]
        j_bottom = (low - first - down * (high - last)) * bottom_g
        j_top = (last + up * (low - first) - high) * top_g
        if not whole:
            rest[0][c] = j_bottom
            rest[0][3 + c] = j_top
            continue
        solved_ref, bottom_ref, top_ref, out_ref, outer_ref, inner_ref = rest
        nz, nx, _ = bottom_ref.shape
        for k in range(nz):
            value = solved_ref[c, k] + bottom_ref[k] * j_bottom - top_ref[k] * j_top
            out_ref[c, k] = value
            store_edges(core, c, k, value[0:1], value[nx - 1 : nx], outer_ref, inner_ref)


def last_kernel(
    solved_ref, bottom_ref, top_ref, j_ref, solved_other, w_other, j_other, out_ref
):
    half = solved_other.shape[1]
    nx = solved_ref.shape[2]
    _, core = chip_and_core()
    mine = pl.ds(pl.multiple_of(core * nx, nx), nx)
    other = pl.ds(pl.multiple_of((1 - core) * nx, nx), nx)
    for c in range(3):
        for k in range(half):
            at = core * half + k
            out_ref[c, k, mine, :] = (
                solved_ref[c, at] + bottom_ref[at] * j_ref[c] - top_ref[at] * j_ref[3 + c]
            )
            out_ref[c, k, other, :] = (
                solved_other[c, k] + w_other[0, k] * j_other[c] - w_other[1, k] * j_other[3 + c]
            )


def per_device(strips, slabs, adjoint, base_flow, conductance, ground_mask, turbine_cells, yaw_bin, yaw_table):
    _, nz, nx, ny = adjoint.shape
    half, chips, levels = nx // 2, slabs // 2, 2 * nz
    cube, field, plane = (levels, half, ny), (3, levels, half, ny), (3, levels, ny)
    cores = [(i, i ^ 1) for i in range(slabs)]
    facing = []
    for strip in range(strips):
        for slab in range(slabs):
            other = strip + (1 if slab % 2 else -1)
            there = other * slabs + (slab ^ 1) if 0 <= other < strips else strip * slabs + (slab ^ 2)
            facing.append((strip * slabs + slab, there))

    def swap(part):
        return lax.ppermute(part, "gz", cores)

    def face(outer):
        return lax.ppermute(outer, ("gx", "gz"), facing)

    def across(parts):
        there = [None] * len(parts)
        for j in range(len(parts), 0, -1):
            pairs = [(i, i ^ (2 * j)) for i in range(slabs)]
            there[j - 1] = lax.ppermute(parts[j - 1], "gz", pairs)
        return there

    def share(whole, after=()):
        shape = (whole.shape[0], nz, half, ny)
        keep, send = call(share_kernel, [shape, shape], (whole,), 0.3, after=after)
        return keep, swap(send)

    part = lambda n: (n, half, ny)
    shape = (nz, half, ny)
    keep, send = call(share_kernel, [(1, *shape)] * 2, (conductance[None],), 0.1)
    extra = -(-nz // half)
    state_keep, state_send, row = call(
        share_kernel,
        [(3, *shape), (3, nz + extra, half, ny), (3, nz, ny)],
        (adjoint,),
        0.3,
        after=[keep],
    )
    ratio, recip, bottom_w, top_w, own, w_send, state_send = call(
        slab_kernel,
        [cube, cube, cube, cube, part(3), (2, nz, half, ny)],
        (keep, swap(send)),
        0.5,
        scratch=[pltpu.VMEM(cube, F32)],
        through=[state_send],
    )
    coefs = across([own] * (chips - 1))
    (source,) = call(
        source_kernel, [field], (turbine_cells, yaw_bin[None], yaw_table), 1.0, after=[own]
    )
    state_recv = swap(state_send)
    state, outer, inner = call(
        gather_state_kernel, [field, plane, plane], (state_keep, state_recv, row), 0.3, after=[source]
    )
    flow_keep, flow_recv = share(base_flow, [own])
    (flow,) = call(gather_kernel, [(2, *cube)], (flow_keep, flow_recv), 0.1)
    for sweep_index in range(SWEEPS):
        first, last = sweep_index == 0, sweep_index == SWEEPS - 1
        outer = face(outer)
        if not first:
            inner = swap(inner)
        extra = [(2, levels, ny), (2, 2, levels, ny)] if first else []
        solved, ends, *extra = call(
            right_kernel,
            [field, part(6), *extra],
            (state, flow, source, ratio, recip, bottom_w, top_w),
            1.5,
        )
        if first:
            edge_w, end_w = extra
            below, above, own_coef = call(
                functools.partial(join_coef_kernel, chips),
                [(chips, half, ny), (chips, half, ny), part(4)],
                (own, *coefs, ground_mask),
                0.1,
                scratch=[pltpu.VMEM((chips, 3, half, ny), F32)],
                after=[ends],
            )
        volts, *parts = call(
            functools.partial(ends_kernel, chips),
            [part(6)] + [part(3)] * (chips - 1),
            (ends, outer, inner, end_w, own_coef),
            0.2,
        )
        others = across(parts)
        solved, *send = call(
            halo_kernel,
            [field] + ([(3, nz, half, ny)] if last else []),
            (solved, outer, inner, edge_w, ratio, recip),
            0.4,
            after=parts[:1],
            scratch=[pltpu.VMEM((3, 2, levels, ny), F32)],
        )
        more = () if last else (solved, bottom_w, top_w)
        outs = call(
            functools.partial(join_kernel, chips, not last),
            [part(6)] if last else [field, plane, plane],
            (*others, volts, below, above, own_coef, *more),
            0.4,
            scratch=[pltpu.VMEM((chips, 3, half, ny), F32)],
        )
        if not last:
            state, outer, inner = outs
    solved_other, w_other = swap(send[0]), swap(w_send)
    (currents,) = outs
    (out,) = call(
        last_kernel,
        [adjoint.shape],
        (solved, bottom_w, top_w, currents, solved_other, w_other, swap(currents)),
        1.0,
    )
    return out


def solution(mesh):
    in_specs = (
        P(None, "gz", "gx", None),
        P(None, "gz", "gx", None),
        P("gz", "gx", None),
        P("gx", None),
        P(),
        P(),
        P(),
    )
    out_specs = P(None, "gz", "gx", None)
    body = functools.partial(per_device, mesh.shape["gx"], mesh.shape["gz"])
    return jax.shard_map(body, mesh=mesh, in_specs=in_specs, out_specs=out_specs, check_vma=False)
```

```python
import functools

import jax
import jax.numpy as jnp
from jax import lax
from jax.experimental import pallas as pl
from jax.experimental.pallas import tpu as pltpu
from jax.sharding import PartitionSpec as P

SWEEPS = 2
PSEUDO_STEP = 0.2
LATERAL_VISC = 1.0


F32 = jnp.float32
VMEM = pl.BlockSpec(memory_space=pltpu.VMEM)
ANY = pl.BlockSpec(memory_space=pl.ANY)


def call(body, outs, ins, cost_us, specs=None, scratch=(), after=(), through=()):
    n, m, k = len(ins), len(ins) + len(after) + len(through), len(through)

    def run(*refs):
        body(*refs[:n], *refs[m : m + len(outs)], *refs[m + len(outs) + k :])

    return pl.pallas_call(
        run,
        out_shape=[jax.ShapeDtypeStruct(s, F32) for s in outs]
        + [jax.ShapeDtypeStruct(t.shape, F32) for t in through],
        in_specs=(specs or [VMEM] * n) + [ANY] * (m - n),
        out_specs=[VMEM] * len(outs) + [ANY] * k,
        input_output_aliases={m - k + i: len(outs) + i for i in range(k)},
        scratch_shapes=list(scratch),
        compiler_params=pltpu.CompilerParams(vmem_limit_bytes=12 * 1024 * 1024),
        cost_estimate=pl.CostEstimate(
            flops=0, bytes_accessed=int(cost_us * 3.0e6), transcendentals=0
        ),
    )(*ins, *after, *through)


def chip_and_core():
    index = lax.axis_index("gz")
    return lax.div(index, 2), lax.rem(index, 2)


def share_kernel(whole_ref, keep_ref, send_ref, *inner_refs):
    parts, nz, nx, _ = whole_ref.shape
    half = nx // 2
    _, core = chip_and_core()
    mine = pl.ds(pl.multiple_of(core * half, half), half)
    other = pl.ds(pl.multiple_of((1 - core) * half, half), half)
    for c in range(parts):
        for k in range(nz):
            keep_ref[c, k] = whole_ref[c, k, mine, :]
            send_ref[c, k] = whole_ref[c, k, other, :]
            if inner_refs:
                before = whole_ref[c, k, half - 1 : half, :]
                behind = whole_ref[c, k, half : half + 1, :]
                at = nz + k // half, slice(k % half, k % half + 1)
                inner_refs[0][c, k : k + 1, :] = jnp.where(core == 0, behind, before)
                send_ref[c, at[0], at[1], :] = jnp.where(core == 0, before, behind)


def store_edges(core, c, k, first, last, outer_ref, inner_ref):
    outer_ref[c, k : k + 1, :] = jnp.where(core == 0, first, last)
    inner_ref[c, k : k + 1, :] = jnp.where(core == 0, last, first)


def gather_kernel(keep_ref, recv_ref, out_ref):
    parts, nz, _, _ = keep_ref.shape
    _, core = chip_and_core()
    for c in range(parts):
        for k in range(nz):
            out_ref[c, core * nz + k] = keep_ref[c, k]
            out_ref[c, (1 - core) * nz + k] = recv_ref[c, k]


def gather_state_kernel(keep_ref, recv_ref, row_ref, out_ref, outer_ref, inner_ref):
    parts, nz, nx, _ = keep_ref.shape
    gather_kernel(keep_ref, recv_ref, out_ref)
    _, core = chip_and_core()
    for c in range(parts):
        inner_ref[c, pl.ds(pl.multiple_of(core * nz, nz), nz), :] = row_ref[c]
        for i in range(nz // nx):
            at = pl.ds(pl.multiple_of((1 - core) * nz + i * nx, nx), nx)
            inner_ref[c, at, :] = recv_ref[c, nz + i]
        for k in range(2 * nz):
            first, last = out_ref[c, k, 0:1, :], out_ref[c, k, nx - 1 : nx, :]
            outer_ref[c, k : k + 1, :] = jnp.where(core == 0, first, last)


def source_kernel(cells_ref, bin_ref, table_ref, source_ref):
    parts, nz, nx, ny = source_ref.shape
    count = cells_ref.shape[1]
    chip, core = chip_and_core()
    lz = cells_ref[0:1, :] - chip * nz
    lx = cells_ref[1:2, :] - (lax.axis_index("gx") * 2 + core) * nx
    inside = (lz >= 0) & (lz < nz) & (lx >= 0) & (lx < nx)
    row = jnp.where(inside, lz * nx + lx, -1)
    at_row = lax.broadcasted_iota(jnp.int32, (nz * nx, count), 0) == row
    at_lane = lax.broadcasted_iota(jnp.int32, (ny, count), 0) == cells_ref[2:3, :]
    at_lane = jnp.where(at_lane, 1.0, 0.0)
    bins = [bin_ref[...] == b for b in range(table_ref.shape[1])]
    for c in range(parts):
        strength = jnp.zeros((1, count), F32)
        for b, here in enumerate(bins):
            strength = jnp.where(here, table_ref[c : c + 1, b : b + 1], strength)
        placed = lax.dot_general(
            jnp.where(at_row, strength, 0.0),
            at_lane,
            (((1,), (1,)), ((), ())),
            precision=lax.Precision.HIGHEST,
            preferred_element_type=F32,
        )
        source_ref[c] = placed.reshape(nz, nx, ny)


def slab_kernel(keep_ref, recv_ref, ratio_ref, recip_ref, bottom_ref, top_ref, own_ref, w_ref, cond_ref):
    nz, nx, ny = cond_ref.shape
    half = nz // 2
    _, core = chip_and_core()
    for k in range(half):
        cond_ref[core * half + k] = keep_ref[0, k]
        cond_ref[(1 - core) * half + k] = recv_ref[0, k]
    sigma = jnp.ones((nx, ny), F32)
    tau = jnp.ones((nx, ny), F32)
    for k in range(nz - 1):
        face = cond_ref[k + 1]
        recip = 1.0 / (sigma + face)
        ratio = face * recip
        recip_ref[k] = recip
        ratio_ref[k + 1] = ratio
        sigma = 1.0 + sigma * ratio
        face = cond_ref[nz - 1 - k]
        ratio = face / (tau + face)
        bottom_ref[nz - 1 - k] = ratio
        tau = 1.0 + tau * ratio
    weight = 1.0 / sigma
    recip_ref[nz - 1] = weight
    ratio_ref[0] = jnp.zeros((nx, ny), F32)
    own_ref[2] = weight
    top_ref[nz - 1] = weight
    for k in range(nz - 2, -1, -1):
        weight = weight * ratio_ref[k + 1]
        top_ref[k] = weight
    own_ref[1] = weight
    weight = 1.0 / tau
    own_ref[0] = weight + 1.0 / cond_ref[0]
    bottom_ref[0] = weight
    for k in range(1, nz):
        weight = weight * bottom_ref[k]
        bottom_ref[k] = weight
    for k in range(half):
        w_ref[0, k] = bottom_ref[(1 - core) * half + k]
        w_ref[1, k] = top_ref[(1 - core) * half + k]


def right_kernel(
    state_ref, flow_ref, source_ref, ratio_ref, recip_ref, bottom_ref, top_ref,
    solved_ref, ends_ref, *edge_refs,
):
    _, nz, nx, ny = state_ref.shape
    lanes = lax.broadcasted_iota(jnp.int32, (nx, ny), 1)
    rows = lax.broadcasted_iota(jnp.int32, (nx, ny), 0)
    visc = PSEUDO_STEP * LATERAL_VISC
    values = [None] * 3
    for k in range(nz):
        u = 0.5 * PSEUDO_STEP * flow_ref[0, k]
        v = 0.5 * PSEUDO_STEP * flow_ref[1, k]
        x_plus_w = visc + u
        x_minus_w = visc - u
        if edge_refs:
            edge_w, end_w = edge_refs
            for side, weight in ((0, x_minus_w[0:1]), (1, x_plus_w[nx - 1 : nx])):
                row = pl.ds(side * (nx - 1), 1)
                edge_w[side, k : k + 1, :] = weight
                end_w[side, 0, k : k + 1, :] = weight * bottom_ref[k, row, :]
                end_w[side, 1, k : k + 1, :] = weight * top_ref[k, row, :]
        x_plus_w = jnp.where(rows == nx - 1, 0.0, x_plus_w)
        x_minus_w = jnp.where(rows == 0, 0.0, x_minus_w)
        y_plus_w = jnp.where(lanes == ny - 1, 0.0, visc + v)
        y_minus_w = jnp.where(lanes == 0, 0.0, visc - v)
        ratio = ratio_ref[k]
        for c in range(3):
            a = state_ref[c, k]
            value = (
                (1.0 - 4.0 * visc) * a
                + x_plus_w * pltpu.roll(a, nx - 1, 0)
                + x_minus_w * pltpu.roll(a, 1, 0)
                + y_plus_w * pltpu.roll(a, ny - 1, 1)
                + y_minus_w * pltpu.roll(a, 1, 1)
                + source_ref[c, k]
            )
            if k:
                value = value + ratio * values[c]
            values[c] = value
            solved_ref[c, k] = value
    for k in range(nz - 1, -1, -1):
        recip = recip_ref[k]
        for c in range(3):
            value = solved_ref[c, k] * recip
            if k < nz - 1:
                value = value + ratio_ref[k + 1] * values[c]
            else:
                ends_ref[3 + c] = value
            values[c] = value
            solved_ref[c, k] = value
    for c in range(3):
        ends_ref[c] = values[c]


def halo_sides(outer_ref, inner_ref, c):
    _, core = chip_and_core()
    strip = lax.axis_index("gx")
    wall = jnp.where(core == 0, strip == 0, strip == lax.axis_size("gx") - 1)
    outer = outer_ref[c] * jnp.where(wall, 0.0, 1.0)
    inner = inner_ref[c]
    return jnp.where(core == 0, outer, inner), jnp.where(core == 0, inner, outer)


def ends_kernel(chips, ends_ref, outer_ref, inner_ref, end_w, own_coef, volt_ref, *parts):
    chip, _ = chip_and_core()
    nx = ends_ref.shape[1]
    rows = lax.broadcasted_iota(jnp.int32, ends_ref.shape[1:], 0)
    up, down = own_coef[0], own_coef[1]
    for c in range(3):
        left, right = halo_sides(outer_ref, inner_ref, c)
        both = []
        for e in range(2):
            low = jnp.sum(left * end_w[0, e], 0, keepdims=True)
            high = jnp.sum(right * end_w[1, e], 0, keepdims=True)
            value = ends_ref[3 * e + c] + jnp.where(rows == 0, low, 0.0)
            value = value + jnp.where(rows == nx - 1, high, 0.0)
            volt_ref[3 * e + c] = value
            both.append(value)
        first, last = both
        to_above = last - up * first
        to_below = first - down * last
        for j in range(1, chips):
            parts[j - 1][c] = jnp.where((chip ^ j) > chip, to_above, to_below)


def halo_kernel(solved_ref, outer_ref, inner_ref, edge_w, ratio_ref, recip_ref, out_ref, *refs):
    _, nz, nx, ny = solved_ref.shape
    right_ref = refs[-1]
    rows = lax.broadcasted_iota(jnp.int32, (nx, ny), 0)
    for c in range(3):
        for side, halo in enumerate(halo_sides(outer_ref, inner_ref, c)):
            right_ref[c, side] = halo * edge_w[side]
    values = [None] * 3
    for k in range(nz):
        ratio = ratio_ref[k]
        for c in range(3):
            value = jnp.where(rows == 0, right_ref[c, 0, k : k + 1, :], 0.0)
            value = jnp.where(rows == nx - 1, right_ref[c, 1, k : k + 1, :], value)
            if k:
                value = value + ratio * values[c]
            values[c] = value
            out_ref[c, k] = value
    for k in range(nz - 1, -1, -1):
        recip = recip_ref[k]
        for c in range(3):
            value = out_ref[c, k] * recip
            if k < nz - 1:
                value = value + ratio_ref[k + 1] * values[c]
            values[c] = value
            out_ref[c, k] = value + solved_ref[c, k]
    if len(refs) > 1:
        half = nz // 2
        _, core = chip_and_core()
        for c in range(3):
            for k in range(half):
                refs[0][c, k] = out_ref[c, (1 - core) * half + k]


def join_coef_kernel(chips, *refs):
    own_ref, others, mask_ref = refs[0], refs[1:chips], refs[chips]
    below_ref, above_ref, own_out, all_ref = refs[chips + 1 :]
    chip, core = chip_and_core()
    nx = own_ref.shape[1]
    all_ref[chip] = own_ref[...]
    for j in range(1, chips):
        all_ref[chip ^ j] = others[j - 1][...]
    mask = mask_ref[pl.ds(pl.multiple_of(core * nx, nx), nx), :].astype(F32)
    zero = jnp.zeros(mask.shape, F32)

    low = zero
    for t in range(chips - 1):
        cross = all_ref[t, 1]
        kappa = cross / (all_ref[t, 0] + low)
        if t == 0:
            kappa = kappa * mask
        below_ref[t] = kappa
        low = jnp.where(t < chip, all_ref[t, 2] - kappa * cross, low)
    below_ref[chips - 1] = zero

    high = zero
    above_ref[chips - 1] = zero
    above_ref[0] = zero
    for t in range(chips - 1, 0, -1):
        cross = all_ref[t, 1]
        kappa = zero if t == chips - 1 else cross / (all_ref[t, 2] + high)
        above_ref[t] = kappa
        high = jnp.where(t > chip, all_ref[t, 0] - kappa * cross, high)

    near, cross, far = own_ref[0], own_ref[1], own_ref[2]
    bottom_on = jnp.where(chip == 0, mask, 1.0)
    top_on = jnp.where(chip == chips - 1, 0.0, 1.0)
    up = cross * bottom_on / (near + low)
    down = cross * top_on / (far + high)
    own_out[0] = up
    own_out[1] = down
    own_out[2] = bottom_on / (low + near - down * cross)
    own_out[3] = top_on / (high + far - up * cross)


def join_kernel(chips, whole, *refs):
    others = refs[: chips - 1]
    volt_ref, below_ref, above_ref, own_coef = refs[chips - 1 : chips + 3]
    rest, all_ref = refs[chips + 3 : -1], refs[-1]
    chip, core = chip_and_core()
    for j in range(1, chips):
        all_ref[chip ^ j] = others[j - 1][...]
    all_ref[chip] = jnp.zeros(all_ref.shape[1:], F32)
    up, down, bottom_g, top_g = (own_coef[i] for i in range(4))
    for c in range(3):
        low = jnp.zeros(up.shape, F32)
        for t in range(chips - 1):
            low = jnp.where(t < chip, all_ref[t, c] + below_ref[t] * low, low)
        high = jnp.zeros(up.shape, F32)
        for t in range(chips - 1, 0, -1):
            high = jnp.where(t > chip, all_ref[t, c] + above_ref[t] * high, high)
        first, last = volt_ref[c], volt_ref[3 + c]
        j_bottom = (low - first - down * (high - last)) * bottom_g
        j_top = (last + up * (low - first) - high) * top_g
        if not whole:
            rest[0][c] = j_bottom
            rest[0][3 + c] = j_top
            continue
        solved_ref, bottom_ref, top_ref, out_ref, outer_ref, inner_ref = rest
        nz, nx, _ = bottom_ref.shape
        for k in range(nz):
            value = solved_ref[c, k] + bottom_ref[k] * j_bottom - top_ref[k] * j_top
            out_ref[c, k] = value
            store_edges(core, c, k, value[0:1], value[nx - 1 : nx], outer_ref, inner_ref)


def last_kernel(
    solved_ref, bottom_ref, top_ref, j_ref, solved_other, w_other, j_other, out_ref
):
    half = solved_other.shape[1]
    nx = solved_ref.shape[2]
    _, core = chip_and_core()
    mine = pl.ds(pl.multiple_of(core * nx, nx), nx)
    other = pl.ds(pl.multiple_of((1 - core) * nx, nx), nx)
    for c in range(3):
        for k in range(half):
            at = core * half + k
            out_ref[c, k, mine, :] = (
                solved_ref[c, at] + bottom_ref[at] * j_ref[c] - top_ref[at] * j_ref[3 + c]
            )
            out_ref[c, k, other, :] = (
                solved_other[c, k] + w_other[0, k] * j_other[c] - w_other[1, k] * j_other[3 + c]
            )


def per_device(strips, slabs, adjoint, base_flow, conductance, ground_mask, turbine_cells, yaw_bin, yaw_table):
    _, nz, nx, ny = adjoint.shape
    half, chips, levels = nx // 2, slabs // 2, 2 * nz
    cube, field, plane = (levels, half, ny), (3, levels, half, ny), (3, levels, ny)
    cores = [(i, i ^ 1) for i in range(slabs)]
    facing = []
    for strip in range(strips):
        for slab in range(slabs):
            other = strip + (1 if slab % 2 else -1)
            there = other * slabs + (slab ^ 1) if 0 <= other < strips else strip * slabs + (slab ^ 2)
            facing.append((strip * slabs + slab, there))

    def swap(part):
        return lax.ppermute(part, "gz", cores)

    def face(outer):
        return lax.ppermute(outer, ("gx", "gz"), facing)

    def across(parts):
        there = [None] * len(parts)
        for j in range(len(parts), 0, -1):
            pairs = [(i, i ^ (2 * j)) for i in range(slabs)]
            there[j - 1] = lax.ppermute(parts[j - 1], "gz", pairs)
        return there

    def share(whole, after=()):
        shape = (whole.shape[0], nz, half, ny)
        keep, send = call(share_kernel, [shape, shape], (whole,), 0.3, after=after)
        return keep, swap(send)

    part = lambda n: (n, half, ny)
    shape = (nz, half, ny)
    extra = -(-nz // half)
    state_keep, state_send, row = call(
        share_kernel,
        [(3, *shape), (3, nz + extra, half, ny), (3, nz, ny)],
        (adjoint,),
        0.3,
    )
    keep, send = call(
        share_kernel, [(1, *shape)] * 2, (conductance[None],), 0.1, after=[state_keep]
    )
    ratio, recip, bottom_w, top_w, own, w_send = call(
        slab_kernel,
        [cube, cube, cube, cube, part(3), (2, nz, half, ny)],
        (keep, swap(send)),
        0.5,
        scratch=[pltpu.VMEM(cube, F32)],
    )
    coefs = across([own] * (chips - 1))
    state_recv = swap(state_send)
    state, outer, inner = call(
        gather_state_kernel,
        [field, plane, plane],
        (state_keep, state_recv, row),
        0.3,
        after=[send],
    )
    (source,) = call(
        source_kernel, [field], (turbine_cells, yaw_bin[None], yaw_table), 1.0, after=[own]
    )
    flow_keep, flow_recv = share(base_flow, [outer])
    (flow,) = call(gather_kernel, [(2, *cube)], (flow_keep, flow_recv), 0.1)
    for sweep_index in range(SWEEPS):
        first, last = sweep_index == 0, sweep_index == SWEEPS - 1
        outer = face(outer)
        if not first:
            inner = swap(inner)
        extra = [(2, levels, ny), (2, 2, levels, ny)] if first else []
        solved, ends, *extra = call(
            right_kernel,
            [field, part(6), *extra],
            (state, flow, source, ratio, recip, bottom_w, top_w),
            1.5,
        )
        if first:
            edge_w, end_w = extra
            below, above, own_coef = call(
                functools.partial(join_coef_kernel, chips),
                [(chips, half, ny), (chips, half, ny), part(4)],
                (own, *coefs, ground_mask),
                0.1,
                scratch=[pltpu.VMEM((chips, 3, half, ny), F32)],
                after=[ends],
            )
        volts, *parts = call(
            functools.partial(ends_kernel, chips),
            [part(6)] + [part(3)] * (chips - 1),
            (ends, outer, inner, end_w, own_coef),
            0.2,
        )
        others = across(parts)
        solved, *send = call(
            halo_kernel,
            [field] + ([(3, nz, half, ny)] if last else []),
            (solved, outer, inner, edge_w, ratio, recip),
            0.4,
            after=parts[:1],
            scratch=[pltpu.VMEM((3, 2, levels, ny), F32)],
        )
        more = () if last else (solved, bottom_w, top_w)
        outs = call(
            functools.partial(join_kernel, chips, not last),
            [part(6)] if last else [field, plane, plane],
            (*others, volts, below, above, own_coef, *more),
            0.4,
            scratch=[pltpu.VMEM((chips, 3, half, ny), F32)],
        )
        if not last:
            state, outer, inner = outs
    solved_other, w_other = swap(send[0]), swap(w_send)
    (currents,) = outs
    (out,) = call(
        last_kernel,
        [adjoint.shape],
        (solved, bottom_w, top_w, currents, solved_other, w_other, swap(currents)),
        1.0,
    )
    return out


def solution(mesh):
    in_specs = (
        P(None, "gz", "gx", None),
        P(None, "gz", "gx", None),
        P("gz", "gx", None),
        P("gx", None),
        P(),
        P(),
        P(),
    )
    out_specs = P(None, "gz", "gx", None)
    body = functools.partial(per_device, mesh.shape["gx"], mesh.shape["gz"])
    return jax.shard_map(body, mesh=mesh, in_specs=in_specs, out_specs=out_specs, check_vma=False)
```

```python
import functools

import jax
import jax.numpy as jnp
from jax import lax
from jax.experimental import pallas as pl
from jax.experimental.pallas import tpu as pltpu
from jax.sharding import PartitionSpec as P

SWEEPS = 2
PSEUDO_STEP = 0.2
LATERAL_VISC = 1.0


F32 = jnp.float32
VMEM = pl.BlockSpec(memory_space=pltpu.VMEM)
ANY = pl.BlockSpec(memory_space=pl.ANY)


def call(body, outs, ins, cost_us, specs=None, scratch=(), after=(), through=()):
    n, m, k = len(ins), len(ins) + len(after) + len(through), len(through)

    def run(*refs):
        body(*refs[:n], *refs[m : m + len(outs)], *refs[m + len(outs) + k :])

    return pl.pallas_call(
        run,
        out_shape=[jax.ShapeDtypeStruct(s, F32) for s in outs]
        + [jax.ShapeDtypeStruct(t.shape, F32) for t in through],
        in_specs=(specs or [VMEM] * n) + [ANY] * (m - n),
        out_specs=[VMEM] * len(outs) + [ANY] * k,
        input_output_aliases={m - k + i: len(outs) + i for i in range(k)},
        scratch_shapes=list(scratch),
        compiler_params=pltpu.CompilerParams(vmem_limit_bytes=12 * 1024 * 1024),
        cost_estimate=pl.CostEstimate(
            flops=0, bytes_accessed=int(cost_us * 3.0e6), transcendentals=0
        ),
    )(*ins, *after, *through)


def chip_and_core():
    index = lax.axis_index("gz")
    return lax.div(index, 2), lax.rem(index, 2)


def share_kernel(whole_ref, keep_ref, send_ref, *inner_refs):
    parts, nz, nx, _ = whole_ref.shape
    half = nx // 2
    _, core = chip_and_core()
    mine = pl.ds(pl.multiple_of(core * half, half), half)
    other = pl.ds(pl.multiple_of((1 - core) * half, half), half)
    for c in range(parts):
        for k in range(nz):
            keep_ref[c, k] = whole_ref[c, k, mine, :]
            send_ref[c, k] = whole_ref[c, k, other, :]
            if inner_refs:
                before = whole_ref[c, k, half - 1 : half, :]
                behind = whole_ref[c, k, half : half + 1, :]
                at = nz + k // half, slice(k % half, k % half + 1)
                inner_refs[0][c, k : k + 1, :] = jnp.where(core == 0, behind, before)
                send_ref[c, at[0], at[1], :] = jnp.where(core == 0, before, behind)
                first, last = whole_ref[c, k, 0:1, :], whole_ref[c, k, nx - 1 : nx, :]
                inner_refs[1][c, k : k + 1, :] = jnp.where(core == 0, first, last)
                inner_refs[2][c, k : k + 1, :] = jnp.where(core == 0, last, first)


def store_edges(core, c, k, first, last, outer_ref, inner_ref):
    outer_ref[c, k : k + 1, :] = jnp.where(core == 0, first, last)
    inner_ref[c, k : k + 1, :] = jnp.where(core == 0, last, first)


def gather_kernel(keep_ref, recv_ref, out_ref):
    parts, nz, _, _ = keep_ref.shape
    _, core = chip_and_core()
    for c in range(parts):
        for k in range(nz):
            out_ref[c, core * nz + k] = keep_ref[c, k]
            out_ref[c, (1 - core) * nz + k] = recv_ref[c, k]


def outer_kernel(keep_ref, recv_ref, outer_ref):
    parts, nz, _ = keep_ref.shape
    _, core = chip_and_core()
    for c in range(parts):
        outer_ref[c, pl.ds(pl.multiple_of(core * nz, nz), nz), :] = keep_ref[c]
        outer_ref[c, pl.ds(pl.multiple_of((1 - core) * nz, nz), nz), :] = recv_ref[c]


def gather_state_kernel(keep_ref, recv_ref, row_ref, out_ref, inner_ref):
    parts, nz, nx, _ = keep_ref.shape
    gather_kernel(keep_ref, recv_ref, out_ref)
    _, core = chip_and_core()
    for c in range(parts):
        inner_ref[c, pl.ds(pl.multiple_of(core * nz, nz), nz), :] = row_ref[c]
        for i in range(nz // nx):
            at = pl.ds(pl.multiple_of((1 - core) * nz + i * nx, nx), nx)
            inner_ref[c, at, :] = recv_ref[c, nz + i]


def source_kernel(cells_ref, bin_ref, table_ref, source_ref):
    parts, nz, nx, ny = source_ref.shape
    count = cells_ref.shape[1]
    chip, core = chip_and_core()
    lz = cells_ref[0:1, :] - chip * nz
    lx = cells_ref[1:2, :] - (lax.axis_index("gx") * 2 + core) * nx
    inside = (lz >= 0) & (lz < nz) & (lx >= 0) & (lx < nx)
    row = jnp.where(inside, lz * nx + lx, -1)
    at_row = lax.broadcasted_iota(jnp.int32, (nz * nx, count), 0) == row
    at_lane = lax.broadcasted_iota(jnp.int32, (ny, count), 0) == cells_ref[2:3, :]
    at_lane = jnp.where(at_lane, 1.0, 0.0)
    bins = [bin_ref[...] == b for b in range(table_ref.shape[1])]
    for c in range(parts):
        strength = jnp.zeros((1, count), F32)
        for b, here in enumerate(bins):
            strength = jnp.where(here, table_ref[c : c + 1, b : b + 1], strength)
        placed = lax.dot_general(
            jnp.where(at_row, strength, 0.0),
            at_lane,
            (((1,), (1,)), ((), ())),
            precision=lax.Precision.HIGHEST,
            preferred_element_type=F32,
        )
        source_ref[c] = placed.reshape(nz, nx, ny)


def slab_kernel(keep_ref, recv_ref, ratio_ref, recip_ref, bottom_ref, top_ref, own_ref, w_ref, cond_ref):
    nz, nx, ny = cond_ref.shape
    half = nz // 2
    _, core = chip_and_core()
    for k in range(half):
        cond_ref[core * half + k] = keep_ref[0, k]
        cond_ref[(1 - core) * half + k] = recv_ref[0, k]
    sigma = jnp.ones((nx, ny), F32)
    tau = jnp.ones((nx, ny), F32)
    for k in range(nz - 1):
        face = cond_ref[k + 1]
        recip = 1.0 / (sigma + face)
        ratio = face * recip
        recip_ref[k] = recip
        ratio_ref[k + 1] = ratio
        sigma = 1.0 + sigma * ratio
        face = cond_ref[nz - 1 - k]
        ratio = face / (tau + face)
        bottom_ref[nz - 1 - k] = ratio
        tau = 1.0 + tau * ratio
    weight = 1.0 / sigma
    recip_ref[nz - 1] = weight
    ratio_ref[0] = jnp.zeros((nx, ny), F32)
    own_ref[2] = weight
    top_ref[nz - 1] = weight
    for k in range(nz - 2, -1, -1):
        weight = weight * ratio_ref[k + 1]
        top_ref[k] = weight
    own_ref[1] = weight
    weight = 1.0 / tau
    own_ref[0] = weight + 1.0 / cond_ref[0]
    bottom_ref[0] = weight
    for k in range(1, nz):
        weight = weight * bottom_ref[k]
        bottom_ref[k] = weight
    for k in range(half):
        w_ref[0, k] = bottom_ref[(1 - core) * half + k]
        w_ref[1, k] = top_ref[(1 - core) * half + k]


def right_kernel(
    state_ref, flow_ref, source_ref, ratio_ref, recip_ref, bottom_ref, top_ref,
    solved_ref, ends_ref, *edge_refs,
):
    _, nz, nx, ny = state_ref.shape
    lanes = lax.broadcasted_iota(jnp.int32, (nx, ny), 1)
    rows = lax.broadcasted_iota(jnp.int32, (nx, ny), 0)
    visc = PSEUDO_STEP * LATERAL_VISC
    values = [None] * 3
    for k in range(nz):
        u = 0.5 * PSEUDO_STEP * flow_ref[0, k]
        v = 0.5 * PSEUDO_STEP * flow_ref[1, k]
        x_plus_w = visc + u
        x_minus_w = visc - u
        if edge_refs:
            edge_w, end_w = edge_refs
            for side, weight in ((0, x_minus_w[0:1]), (1, x_plus_w[nx - 1 : nx])):
                row = pl.ds(side * (nx - 1), 1)
                edge_w[side, k : k + 1, :] = weight
                end_w[side, 0, k : k + 1, :] = weight * bottom_ref[k, row, :]
                end_w[side, 1, k : k + 1, :] = weight * top_ref[k, row, :]
        x_plus_w = jnp.where(rows == nx - 1, 0.0, x_plus_w)
        x_minus_w = jnp.where(rows == 0, 0.0, x_minus_w)
        y_plus_w = jnp.where(lanes == ny - 1, 0.0, visc + v)
        y_minus_w = jnp.where(lanes == 0, 0.0, visc - v)
        ratio = ratio_ref[k]
        for c in range(3):
            a = state_ref[c, k]
            value = (
                (1.0 - 4.0 * visc) * a
                + x_plus_w * pltpu.roll(a, nx - 1, 0)
                + x_minus_w * pltpu.roll(a, 1, 0)
                + y_plus_w * pltpu.roll(a, ny - 1, 1)
                + y_minus_w * pltpu.roll(a, 1, 1)
                + source_ref[c, k]
            )
            if k:
                value = value + ratio * values[c]
            values[c] = value
            solved_ref[c, k] = value
    for k in range(nz - 1, -1, -1):
        recip = recip_ref[k]
        for c in range(3):
            value = solved_ref[c, k] * recip
            if k < nz - 1:
                value = value + ratio_ref[k + 1] * values[c]
            else:
                ends_ref[3 + c] = value
            values[c] = value
            solved_ref[c, k] = value
    for c in range(3):
        ends_ref[c] = values[c]


def halo_sides(outer_ref, inner_ref, c):
    _, core = chip_and_core()
    strip = lax.axis_index("gx")
    wall = jnp.where(core == 0, strip == 0, strip == lax.axis_size("gx") - 1)
    outer = outer_ref[c] * jnp.where(wall, 0.0, 1.0)
    inner = inner_ref[c]
    return jnp.where(core == 0, outer, inner), jnp.where(core == 0, inner, outer)


def ends_kernel(chips, ends_ref, outer_ref, inner_ref, end_w, own_coef, volt_ref, *parts):
    chip, _ = chip_and_core()
    nx = ends_ref.shape[1]
    rows = lax.broadcasted_iota(jnp.int32, ends_ref.shape[1:], 0)
    up, down = own_coef[0], own_coef[1]
    for c in range(3):
        left, right = halo_sides(outer_ref, inner_ref, c)
        both = []
        for e in range(2):
            low = jnp.sum(left * end_w[0, e], 0, keepdims=True)
            high = jnp.sum(right * end_w[1, e], 0, keepdims=True)
            value = ends_ref[3 * e + c] + jnp.where(rows == 0, low, 0.0)
            value = value + jnp.where(rows == nx - 1, high, 0.0)
            volt_ref[3 * e + c] = value
            both.append(value)
        first, last = both
        to_above = last - up * first
        to_below = first - down * last
        for j in range(1, chips):
            parts[j - 1][c] = jnp.where((chip ^ j) > chip, to_above, to_below)


def halo_kernel(solved_ref, outer_ref, inner_ref, edge_w, ratio_ref, recip_ref, out_ref, *refs):
    _, nz, nx, ny = solved_ref.shape
    right_ref = refs[-1]
    rows = lax.broadcasted_iota(jnp.int32, (nx, ny), 0)
    for c in range(3):
        for side, halo in enumerate(halo_sides(outer_ref, inner_ref, c)):
            right_ref[c, side] = halo * edge_w[side]
    values = [None] * 3
    for k in range(nz):
        ratio = ratio_ref[k]
        for c in range(3):
            value = jnp.where(rows == 0, right_ref[c, 0, k : k + 1, :], 0.0)
            value = jnp.where(rows == nx - 1, right_ref[c, 1, k : k + 1, :], value)
            if k:
                value = value + ratio * values[c]
            values[c] = value
            out_ref[c, k] = value
    for k in range(nz - 1, -1, -1):
        recip = recip_ref[k]
        for c in range(3):
            value = out_ref[c, k] * recip
            if k < nz - 1:
                value = value + ratio_ref[k + 1] * values[c]
            values[c] = value
            out_ref[c, k] = value + solved_ref[c, k]
    if len(refs) > 1:
        half = nz // 2
        _, core = chip_and_core()
        for c in range(3):
            for k in range(half):
                refs[0][c, k] = out_ref[c, (1 - core) * half + k]


def join_coef_kernel(chips, *refs):
    own_ref, others, mask_ref = refs[0], refs[1:chips], refs[chips]
    below_ref, above_ref, own_out, all_ref = refs[chips + 1 :]
    chip, core = chip_and_core()
    nx = own_ref.shape[1]
    all_ref[chip] = own_ref[...]
    for j in range(1, chips):
        all_ref[chip ^ j] = others[j - 1][...]
    mask = mask_ref[pl.ds(pl.multiple_of(core * nx, nx), nx), :].astype(F32)
    zero = jnp.zeros(mask.shape, F32)

    low = zero
    for t in range(chips - 1):
        cross = all_ref[t, 1]
        kappa = cross / (all_ref[t, 0] + low)
        if t == 0:
            kappa = kappa * mask
        below_ref[t] = kappa
        low = jnp.where(t < chip, all_ref[t, 2] - kappa * cross, low)
    below_ref[chips - 1] = zero

    high = zero
    above_ref[chips - 1] = zero
    above_ref[0] = zero
    for t in range(chips - 1, 0, -1):
        cross = all_ref[t, 1]
        kappa = zero if t == chips - 1 else cross / (all_ref[t, 2] + high)
        above_ref[t] = kappa
        high = jnp.where(t > chip, all_ref[t, 0] - kappa * cross, high)

    near, cross, far = own_ref[0], own_ref[1], own_ref[2]
    bottom_on = jnp.where(chip == 0, mask, 1.0)
    top_on = jnp.where(chip == chips - 1, 0.0, 1.0)
    up = cross * bottom_on / (near + low)
    down = cross * top_on / (far + high)
    own_out[0] = up
    own_out[1] = down
    own_out[2] = bottom_on / (low + near - down * cross)
    own_out[3] = top_on / (high + far - up * cross)


def join_kernel(chips, whole, *refs):
    others = refs[: chips - 1]
    volt_ref, below_ref, above_ref, own_coef = refs[chips - 1 : chips + 3]
    rest, all_ref = refs[chips + 3 : -1], refs[-1]
    chip, core = chip_and_core()
    for j in range(1, chips):
        all_ref[chip ^ j] = others[j - 1][...]
    all_ref[chip] = jnp.zeros(all_ref.shape[1:], F32)
    up, down, bottom_g, top_g = (own_coef[i] for i in range(4))
    for c in range(3):
        low = jnp.zeros(up.shape, F32)
        for t in range(chips - 1):
            low = jnp.where(t < chip, all_ref[t, c] + below_ref[t] * low, low)
        high = jnp.zeros(up.shape, F32)
        for t in range(chips - 1, 0, -1):
            high = jnp.where(t > chip, all_ref[t, c] + above_ref[t] * high, high)
        first, last = volt_ref[c], volt_ref[3 + c]
        j_bottom = (low - first - down * (high - last)) * bottom_g
        j_top = (last + up * (low - first) - high) * top_g
        if not whole:
            rest[0][c] = j_bottom
            rest[0][3 + c] = j_top
            continue
        solved_ref, bottom_ref, top_ref, out_ref, outer_ref, inner_ref = rest
        nz, nx, _ = bottom_ref.shape
        for k in range(nz):
            value = solved_ref[c, k] + bottom_ref[k] * j_bottom - top_ref[k] * j_top
            out_ref[c, k] = value
            store_edges(core, c, k, value[0:1], value[nx - 1 : nx], outer_ref, inner_ref)


def last_kernel(
    solved_ref, bottom_ref, top_ref, j_ref, solved_other, w_other, j_other, out_ref
):
    half = solved_other.shape[1]
    nx = solved_ref.shape[2]
    _, core = chip_and_core()
    mine = pl.ds(pl.multiple_of(core * nx, nx), nx)
    other = pl.ds(pl.multiple_of((1 - core) * nx, nx), nx)
    for c in range(3):
        for k in range(half):
            at = core * half + k
            out_ref[c, k, mine, :] = (
                solved_ref[c, at] + bottom_ref[at] * j_ref[c] - top_ref[at] * j_ref[3 + c]
            )
            out_ref[c, k, other, :] = (
                solved_other[c, k] + w_other[0, k] * j_other[c] - w_other[1, k] * j_other[3 + c]
            )


def per_device(strips, slabs, adjoint, base_flow, conductance, ground_mask, turbine_cells, yaw_bin, yaw_table):
    _, nz, nx, ny = adjoint.shape
    half, chips, levels = nx // 2, slabs // 2, 2 * nz
    cube, field, plane = (levels, half, ny), (3, levels, half, ny), (3, levels, ny)
    cores = [(i, i ^ 1) for i in range(slabs)]
    facing = []
    for strip in range(strips):
        for slab in range(slabs):
            other = strip + (1 if slab % 2 else -1)
            there = other * slabs + (slab ^ 1) if 0 <= other < strips else strip * slabs + (slab ^ 2)
            facing.append((strip * slabs + slab, there))

    def swap(part):
        return lax.ppermute(part, "gz", cores)

    def face(outer):
        return lax.ppermute(outer, ("gx", "gz"), facing)

    def across(parts, far=True):
        there = [None] * len(parts)
        for j in sorted(range(1, len(parts) + 1), reverse=far):
            pairs = [(i, i ^ (2 * j)) for i in range(slabs)]
            there[j - 1] = lax.ppermute(parts[j - 1], "gz", pairs)
        return there

    def share(whole, after=()):
        shape = (whole.shape[0], nz, half, ny)
        keep, send = call(share_kernel, [shape, shape], (whole,), 0.3, after=after)
        return keep, swap(send)

    part = lambda n: (n, half, ny)
    shape = (nz, half, ny)
    extra = -(-nz // half)
    state_keep, state_send, row, edge_keep, edge_send = call(
        share_kernel,
        [(3, *shape), (3, nz + extra, half, ny)] + [(3, nz, ny)] * 3,
        (adjoint,),
        0.3,
    )
    keep, send = call(
        share_kernel, [(1, *shape)] * 2, (conductance[None],), 0.1, after=[state_keep]
    )
    outer, state_send = call(
        outer_kernel, [plane], (edge_keep, swap(edge_send)), 0.1,
        after=[send], through=[state_send],
    )
    ratio, recip, bottom_w, top_w, own, w_send = call(
        slab_kernel,
        [cube, cube, cube, cube, part(3), (2, nz, half, ny)],
        (keep, swap(send)),
        0.5,
        scratch=[pltpu.VMEM(cube, F32)],
    )
    coefs = across([own] * (chips - 1), False)
    state_recv = swap(state_send)
    state, inner = call(
        gather_state_kernel, [field, plane], (state_keep, state_recv, row), 0.3
    )
    (source,) = call(
        source_kernel, [field], (turbine_cells, yaw_bin[None], yaw_table), 1.0, after=[own]
    )
    flow_keep, flow_recv = share(base_flow, [outer])
    (flow,) = call(gather_kernel, [(2, *cube)], (flow_keep, flow_recv), 0.1)
    for sweep_index in range(SWEEPS):
        first, last = sweep_index == 0, sweep_index == SWEEPS - 1
        outer = face(outer)
        if not first:
            inner = swap(inner)
        extra = [(2, levels, ny), (2, 2, levels, ny)] if first else []
        solved, ends, *extra = call(
            right_kernel,
            [field, part(6), *extra],
            (state, flow, source, ratio, recip, bottom_w, top_w),
            1.5,
        )
        if first:
            edge_w, end_w = extra
            below, above, own_coef = call(
                functools.partial(join_coef_kernel, chips),
                [(chips, half, ny), (chips, half, ny), part(4)],
                (own, *coefs, ground_mask),
                0.1,
                scratch=[pltpu.VMEM((chips, 3, half, ny), F32)],
                after=[ends],
            )
        volts, *parts = call(
            functools.partial(ends_kernel, chips),
            [part(6)] + [part(3)] * (chips - 1),
            (ends, outer, inner, end_w, own_coef),
            0.2,
        )
        others = across(parts)
        solved, *send = call(
            halo_kernel,
            [field] + ([(3, nz, half, ny)] if last else []),
            (solved, outer, inner, edge_w, ratio, recip),
            0.4,
            after=parts[:1],
            scratch=[pltpu.VMEM((3, 2, levels, ny), F32)],
        )
        more = () if last else (solved, bottom_w, top_w)
        outs = call(
            functools.partial(join_kernel, chips, not last),
            [part(6)] if last else [field, plane, plane],
            (*others, volts, below, above, own_coef, *more),
            0.4,
            scratch=[pltpu.VMEM((chips, 3, half, ny), F32)],
        )
        if not last:
            state, outer, inner = outs
    solved_other, w_other = swap(send[0]), swap(w_send)
    (currents,) = outs
    (out,) = call(
        last_kernel,
        [adjoint.shape],
        (solved, bottom_w, top_w, currents, solved_other, w_other, swap(currents)),
        1.0,
    )
    return out


def solution(mesh):
    in_specs = (
        P(None, "gz", "gx", None),
        P(None, "gz", "gx", None),
        P("gz", "gx", None),
        P("gx", None),
        P(),
        P(),
        P(),
    )
    out_specs = P(None, "gz", "gx", None)
    body = functools.partial(per_device, mesh.shape["gx"], mesh.shape["gz"])
    return jax.shard_map(body, mesh=mesh, in_specs=in_specs, out_specs=out_specs, check_vma=False)
```

```python
import functools

import jax
import jax.numpy as jnp
from jax import lax
from jax.experimental import pallas as pl
from jax.experimental.pallas import tpu as pltpu
from jax.sharding import PartitionSpec as P

SWEEPS = 2
PSEUDO_STEP = 0.2
LATERAL_VISC = 1.0


F32 = jnp.float32
VMEM = pl.BlockSpec(memory_space=pltpu.VMEM)
ANY = pl.BlockSpec(memory_space=pl.ANY)


def call(body, outs, ins, cost_us, specs=None, scratch=(), after=(), through=()):
    n, m, k = len(ins), len(ins) + len(after) + len(through), len(through)

    def run(*refs):
        body(*refs[:n], *refs[m : m + len(outs)], *refs[m + len(outs) + k :])

    return pl.pallas_call(
        run,
        out_shape=[jax.ShapeDtypeStruct(s, F32) for s in outs]
        + [jax.ShapeDtypeStruct(t.shape, F32) for t in through],
        in_specs=(specs or [VMEM] * n) + [ANY] * (m - n),
        out_specs=[VMEM] * len(outs) + [ANY] * k,
        input_output_aliases={m - k + i: len(outs) + i for i in range(k)},
        scratch_shapes=list(scratch),
        compiler_params=pltpu.CompilerParams(vmem_limit_bytes=12 * 1024 * 1024),
        cost_estimate=pl.CostEstimate(
            flops=0, bytes_accessed=int(cost_us * 3.0e6), transcendentals=0
        ),
    )(*ins, *after, *through)


def chip_and_core():
    index = lax.axis_index("gz")
    return lax.div(index, 2), lax.rem(index, 2)


def share_kernel(whole_ref, keep_ref, send_ref, *inner_refs):
    parts, nz, nx, _ = whole_ref.shape
    half = nx // 2
    _, core = chip_and_core()
    mine = pl.ds(pl.multiple_of(core * half, half), half)
    other = pl.ds(pl.multiple_of((1 - core) * half, half), half)
    for c in range(parts):
        for k in range(nz):
            keep_ref[c, k] = whole_ref[c, k, mine, :]
            send_ref[c, k] = whole_ref[c, k, other, :]
            if inner_refs:
                before = whole_ref[c, k, half - 1 : half, :]
                behind = whole_ref[c, k, half : half + 1, :]
                at = nz + k // half, slice(k % half, k % half + 1)
                inner_refs[0][c, k : k + 1, :] = jnp.where(core == 0, behind, before)
                send_ref[c, at[0], at[1], :] = jnp.where(core == 0, before, behind)
                first, last = whole_ref[c, k, 0:1, :], whole_ref[c, k, nx - 1 : nx, :]
                inner_refs[1][c, k : k + 1, :] = jnp.where(core == 0, first, last)
                inner_refs[2][c, k : k + 1, :] = jnp.where(core == 0, last, first)


def store_edges(core, c, k, first, last, outer_ref, inner_ref):
    outer_ref[c, k : k + 1, :] = jnp.where(core == 0, first, last)
    inner_ref[c, k : k + 1, :] = jnp.where(core == 0, last, first)


def gather_kernel(keep_ref, recv_ref, out_ref):
    parts, nz, _, _ = keep_ref.shape
    _, core = chip_and_core()
    for c in range(parts):
        for k in range(nz):
            out_ref[c, core * nz + k] = keep_ref[c, k]
            out_ref[c, (1 - core) * nz + k] = recv_ref[c, k]


def outer_kernel(keep_ref, recv_ref, outer_ref):
    parts, nz, _ = keep_ref.shape
    _, core = chip_and_core()
    for c in range(parts):
        outer_ref[c, pl.ds(pl.multiple_of(core * nz, nz), nz), :] = keep_ref[c]
        outer_ref[c, pl.ds(pl.multiple_of((1 - core) * nz, nz), nz), :] = recv_ref[c]


def gather_state_kernel(keep_ref, recv_ref, row_ref, out_ref, inner_ref):
    parts, nz, nx, _ = keep_ref.shape
    gather_kernel(keep_ref, recv_ref, out_ref)
    _, core = chip_and_core()
    for c in range(parts):
        inner_ref[c, pl.ds(pl.multiple_of(core * nz, nz), nz), :] = row_ref[c]
        for i in range(nz // nx):
            at = pl.ds(pl.multiple_of((1 - core) * nz + i * nx, nx), nx)
            inner_ref[c, at, :] = recv_ref[c, nz + i]


def source_kernel(cells_ref, bin_ref, table_ref, source_ref):
    parts, nz, nx, ny = source_ref.shape
    count = cells_ref.shape[1]
    chip, core = chip_and_core()
    lz = cells_ref[0:1, :] - chip * nz
    lx = cells_ref[1:2, :] - (lax.axis_index("gx") * 2 + core) * nx
    inside = (lz >= 0) & (lz < nz) & (lx >= 0) & (lx < nx)
    row = jnp.where(inside, lz * nx + lx, -1)
    at_row = lax.broadcasted_iota(jnp.int32, (nz * nx, count), 0) == row
    at_lane = lax.broadcasted_iota(jnp.int32, (ny, count), 0) == cells_ref[2:3, :]
    at_lane = jnp.where(at_lane, 1.0, 0.0)
    bins = [bin_ref[...] == b for b in range(table_ref.shape[1])]
    for c in range(parts):
        strength = jnp.zeros((1, count), F32)
        for b, here in enumerate(bins):
            strength = jnp.where(here, table_ref[c : c + 1, b : b + 1], strength)
        placed = lax.dot_general(
            jnp.where(at_row, strength, 0.0),
            at_lane,
            (((1,), (1,)), ((), ())),
            precision=lax.Precision.HIGHEST,
            preferred_element_type=F32,
        )
        source_ref[c] = placed.reshape(nz, nx, ny)


def slab_kernel(keep_ref, recv_ref, ratio_ref, recip_ref, bottom_ref, top_ref, own_ref, w_ref, cond_ref):
    nz, nx, ny = cond_ref.shape
    half = nz // 2
    _, core = chip_and_core()
    for k in range(half):
        cond_ref[core * half + k] = keep_ref[0, k]
        cond_ref[(1 - core) * half + k] = recv_ref[0, k]
    sigma = jnp.ones((nx, ny), F32)
    tau = jnp.ones((nx, ny), F32)
    for k in range(nz - 1):
        face = cond_ref[k + 1]
        recip = 1.0 / (sigma + face)
        ratio = face * recip
        recip_ref[k] = recip
        ratio_ref[k + 1] = ratio
        sigma = 1.0 + sigma * ratio
        face = cond_ref[nz - 1 - k]
        ratio = face / (tau + face)
        bottom_ref[nz - 1 - k] = ratio
        tau = 1.0 + tau * ratio
    weight = 1.0 / sigma
    recip_ref[nz - 1] = weight
    ratio_ref[0] = jnp.zeros((nx, ny), F32)
    own_ref[2] = weight
    top_ref[nz - 1] = weight
    for k in range(nz - 2, -1, -1):
        weight = weight * ratio_ref[k + 1]
        top_ref[k] = weight
    own_ref[1] = weight
    weight = 1.0 / tau
    own_ref[0] = weight + 1.0 / cond_ref[0]
    bottom_ref[0] = weight
    for k in range(1, nz):
        weight = weight * bottom_ref[k]
        bottom_ref[k] = weight
    for k in range(half):
        w_ref[0, k] = bottom_ref[(1 - core) * half + k]
        w_ref[1, k] = top_ref[(1 - core) * half + k]


def right_kernel(
    state_ref, flow_ref, source_ref, ratio_ref, recip_ref, bottom_ref, top_ref,
    solved_ref, ends_ref, *edge_refs,
):
    _, nz, nx, ny = state_ref.shape
    lanes = lax.broadcasted_iota(jnp.int32, (nx, ny), 1)
    rows = lax.broadcasted_iota(jnp.int32, (nx, ny), 0)
    visc = PSEUDO_STEP * LATERAL_VISC
    values = [None] * 3
    for k in range(nz):
        u = 0.5 * PSEUDO_STEP * flow_ref[0, k]
        v = 0.5 * PSEUDO_STEP * flow_ref[1, k]
        x_plus_w = visc + u
        x_minus_w = visc - u
        if edge_refs:
            edge_w, end_w = edge_refs
            for side, weight in ((0, x_minus_w[0:1]), (1, x_plus_w[nx - 1 : nx])):
                row = pl.ds(side * (nx - 1), 1)
                edge_w[side, k : k + 1, :] = weight
                end_w[side, 0, k : k + 1, :] = weight * bottom_ref[k, row, :]
                end_w[side, 1, k : k + 1, :] = weight * top_ref[k, row, :]
        x_plus_w = jnp.where(rows == nx - 1, 0.0, x_plus_w)
        x_minus_w = jnp.where(rows == 0, 0.0, x_minus_w)
        y_plus_w = jnp.where(lanes == ny - 1, 0.0, visc + v)
        y_minus_w = jnp.where(lanes == 0, 0.0, visc - v)
        ratio = ratio_ref[k]
        for c in range(3):
            a = state_ref[c, k]
            value = (
                (1.0 - 4.0 * visc) * a
                + x_plus_w * pltpu.roll(a, nx - 1, 0)
                + x_minus_w * pltpu.roll(a, 1, 0)
                + y_plus_w * pltpu.roll(a, ny - 1, 1)
                + y_minus_w * pltpu.roll(a, 1, 1)
                + source_ref[c, k]
            )
            if k:
                value = value + ratio * values[c]
            values[c] = value
            solved_ref[c, k] = value
    for k in range(nz - 1, -1, -1):
        recip = recip_ref[k]
        for c in range(3):
            value = solved_ref[c, k] * recip
            if k < nz - 1:
                value = value + ratio_ref[k + 1] * values[c]
            else:
                ends_ref[3 + c] = value
            values[c] = value
            solved_ref[c, k] = value
    for c in range(3):
        ends_ref[c] = values[c]


def halo_sides(outer_ref, inner_ref, c):
    _, core = chip_and_core()
    strip = lax.axis_index("gx")
    wall = jnp.where(core == 0, strip == 0, strip == lax.axis_size("gx") - 1)
    outer = outer_ref[c] * jnp.where(wall, 0.0, 1.0)
    inner = inner_ref[c]
    return jnp.where(core == 0, outer, inner), jnp.where(core == 0, inner, outer)


def ends_kernel(chips, ends_ref, outer_ref, inner_ref, end_w, own_coef, volt_ref, *parts):
    chip, _ = chip_and_core()
    nx = ends_ref.shape[1]
    rows = lax.broadcasted_iota(jnp.int32, ends_ref.shape[1:], 0)
    up, down = own_coef[0], own_coef[1]
    for c in range(3):
        left, right = halo_sides(outer_ref, inner_ref, c)
        both = []
        for e in range(2):
            low = jnp.sum(left * end_w[0, e], 0, keepdims=True)
            high = jnp.sum(right * end_w[1, e], 0, keepdims=True)
            value = ends_ref[3 * e + c] + jnp.where(rows == 0, low, 0.0)
            value = value + jnp.where(rows == nx - 1, high, 0.0)
            volt_ref[3 * e + c] = value
            both.append(value)
        first, last = both
        to_above = last - up * first
        to_below = first - down * last
        for j in range(1, chips):
            parts[j - 1][c] = jnp.where((chip ^ j) > chip, to_above, to_below)


def halo_kernel(solved_ref, outer_ref, inner_ref, edge_w, ratio_ref, recip_ref, out_ref, *refs):
    _, nz, nx, ny = solved_ref.shape
    right_ref = refs[-1]
    rows = lax.broadcasted_iota(jnp.int32, (nx, ny), 0)
    for c in range(3):
        for side, halo in enumerate(halo_sides(outer_ref, inner_ref, c)):
            right_ref[c, side] = halo * edge_w[side]
    values = [None] * 3
    for k in range(nz):
        ratio = ratio_ref[k]
        for c in range(3):
            value = jnp.where(rows == 0, right_ref[c, 0, k : k + 1, :], 0.0)
            value = jnp.where(rows == nx - 1, right_ref[c, 1, k : k + 1, :], value)
            if k:
                value = value + ratio * values[c]
            values[c] = value
            out_ref[c, k] = value
    for k in range(nz - 1, -1, -1):
        recip = recip_ref[k]
        for c in range(3):
            value = out_ref[c, k] * recip
            if k < nz - 1:
                value = value + ratio_ref[k + 1] * values[c]
            values[c] = value
            out_ref[c, k] = value + solved_ref[c, k]
    if len(refs) > 1:
        half = nz // 2
        _, core = chip_and_core()
        for c in range(3):
            for k in range(half):
                refs[0][c, k] = out_ref[c, (1 - core) * half + k]


def join_coef_kernel(chips, *refs):
    own_ref, others, mask_ref = refs[0], refs[1:chips], refs[chips]
    below_ref, above_ref, own_out, all_ref = refs[chips + 1 :]
    chip, core = chip_and_core()
    nx = own_ref.shape[1]
    all_ref[chip] = own_ref[...]
    for j in range(1, chips):
        all_ref[chip ^ j] = others[j - 1][...]
    mask = mask_ref[pl.ds(pl.multiple_of(core * nx, nx), nx), :].astype(F32)
    zero = jnp.zeros(mask.shape, F32)

    low = zero
    for t in range(chips - 1):
        cross = all_ref[t, 1]
        kappa = cross / (all_ref[t, 0] + low)
        if t == 0:
            kappa = kappa * mask
        below_ref[t] = kappa
        low = jnp.where(t < chip, all_ref[t, 2] - kappa * cross, low)
    below_ref[chips - 1] = zero

    high = zero
    above_ref[chips - 1] = zero
    above_ref[0] = zero
    for t in range(chips - 1, 0, -1):
        cross = all_ref[t, 1]
        kappa = zero if t == chips - 1 else cross / (all_ref[t, 2] + high)
        above_ref[t] = kappa
        high = jnp.where(t > chip, all_ref[t, 0] - kappa * cross, high)

    near, cross, far = own_ref[0], own_ref[1], own_ref[2]
    bottom_on = jnp.where(chip == 0, mask, 1.0)
    top_on = jnp.where(chip == chips - 1, 0.0, 1.0)
    up = cross * bottom_on / (near + low)
    down = cross * top_on / (far + high)
    own_out[0] = up
    own_out[1] = down
    own_out[2] = bottom_on / (low + near - down * cross)
    own_out[3] = top_on / (high + far - up * cross)


def join_kernel(chips, whole, *refs):
    others = refs[: chips - 1]
    volt_ref, below_ref, above_ref, own_coef = refs[chips - 1 : chips + 3]
    rest, all_ref = refs[chips + 3 : -1], refs[-1]
    chip, core = chip_and_core()
    for j in range(1, chips):
        all_ref[chip ^ j] = others[j - 1][...]
    all_ref[chip] = jnp.zeros(all_ref.shape[1:], F32)
    up, down, bottom_g, top_g = (own_coef[i] for i in range(4))
    for c in range(3):
        low = jnp.zeros(up.shape, F32)
        for t in range(chips - 1):
            low = jnp.where(t < chip, all_ref[t, c] + below_ref[t] * low, low)
        high = jnp.zeros(up.shape, F32)
        for t in range(chips - 1, 0, -1):
            high = jnp.where(t > chip, all_ref[t, c] + above_ref[t] * high, high)
        first, last = volt_ref[c], volt_ref[3 + c]
        j_bottom = (low - first - down * (high - last)) * bottom_g
        j_top = (last + up * (low - first) - high) * top_g
        if not whole:
            rest[0][c] = j_bottom
            rest[0][3 + c] = j_top
            continue
        solved_ref, bottom_ref, top_ref, out_ref, outer_ref, inner_ref = rest
        nz, nx, _ = bottom_ref.shape
        for k in range(nz):
            value = solved_ref[c, k] + bottom_ref[k] * j_bottom - top_ref[k] * j_top
            out_ref[c, k] = value
            store_edges(core, c, k, value[0:1], value[nx - 1 : nx], outer_ref, inner_ref)


def last_kernel(
    solved_ref, bottom_ref, top_ref, j_ref, solved_other, w_other, j_other, out_ref
):
    half = solved_other.shape[1]
    nx = solved_ref.shape[2]
    _, core = chip_and_core()
    mine = pl.ds(pl.multiple_of(core * nx, nx), nx)
    other = pl.ds(pl.multiple_of((1 - core) * nx, nx), nx)
    for c in range(3):
        for k in range(half):
            at = core * half + k
            out_ref[c, k, mine, :] = (
                solved_ref[c, at] + bottom_ref[at] * j_ref[c] - top_ref[at] * j_ref[3 + c]
            )
            out_ref[c, k, other, :] = (
                solved_other[c, k] + w_other[0, k] * j_other[c] - w_other[1, k] * j_other[3 + c]
            )


def per_device(strips, slabs, adjoint, base_flow, conductance, ground_mask, turbine_cells, yaw_bin, yaw_table):
    _, nz, nx, ny = adjoint.shape
    half, chips, levels = nx // 2, slabs // 2, 2 * nz
    cube, field, plane = (levels, half, ny), (3, levels, half, ny), (3, levels, ny)
    cores = [(i, i ^ 1) for i in range(slabs)]
    facing = []
    for strip in range(strips):
        for slab in range(slabs):
            other = strip + (1 if slab % 2 else -1)
            there = other * slabs + (slab ^ 1) if 0 <= other < strips else strip * slabs + (slab ^ 2)
            facing.append((strip * slabs + slab, there))

    def swap(part):
        return lax.ppermute(part, "gz", cores)

    def face(outer):
        return lax.ppermute(outer, ("gx", "gz"), facing)

    def across(parts, far=True):
        there = [None] * len(parts)
        for j in sorted(range(1, len(parts) + 1), reverse=far):
            pairs = [(i, i ^ (2 * j)) for i in range(slabs)]
            there[j - 1] = lax.ppermute(parts[j - 1], "gz", pairs)
        return there

    def share(whole, after=()):
        shape = (whole.shape[0], nz, half, ny)
        keep, send = call(share_kernel, [shape, shape], (whole,), 0.3, after=after)
        return keep, swap(send)

    part = lambda n: (n, half, ny)
    shape = (nz, half, ny)
    extra = -(-nz // half)
    state_keep, state_send, row, edge_keep, edge_send = call(
        share_kernel,
        [(3, *shape), (3, nz + extra, half, ny)] + [(3, nz, ny)] * 3,
        (adjoint,),
        0.3,
    )
    keep, send = call(
        share_kernel, [(1, *shape)] * 2, (conductance[None],), 0.1, after=[state_keep]
    )
    outer, state_send = call(
        outer_kernel, [plane], (edge_keep, swap(edge_send)), 0.1,
        after=[send], through=[state_send],
    )
    ratio, recip, bottom_w, top_w, own, w_send = call(
        slab_kernel,
        [cube, cube, cube, cube, part(3), (2, nz, half, ny)],
        (keep, swap(send)),
        0.5,
        scratch=[pltpu.VMEM(cube, F32)],
    )
    coefs = across([own] * (chips - 1), False)
    state_recv = swap(state_send)
    state, inner = call(
        gather_state_kernel, [field, plane], (state_keep, state_recv, row), 0.3
    )
    (source,) = call(
        source_kernel, [field], (turbine_cells, yaw_bin[None], yaw_table), 1.0
    )
    flow_keep, flow_recv = share(base_flow, [outer])
    (flow,) = call(gather_kernel, [(2, *cube)], (flow_keep, flow_recv), 0.1)
    for sweep_index in range(SWEEPS):
        first, last = sweep_index == 0, sweep_index == SWEEPS - 1
        outer = face(outer)
        if not first:
            inner = swap(inner)
        extra = [(2, levels, ny), (2, 2, levels, ny)] if first else []
        solved, ends, *extra = call(
            right_kernel,
            [field, part(6), *extra],
            (state, flow, source, ratio, recip, bottom_w, top_w),
            1.5,
        )
        if first:
            edge_w, end_w = extra
            below, above, own_coef = call(
                functools.partial(join_coef_kernel, chips),
                [(chips, half, ny), (chips, half, ny), part(4)],
                (own, *coefs, ground_mask),
                0.1,
                scratch=[pltpu.VMEM((chips, 3, half, ny), F32)],
                after=[ends],
            )
        volts, *parts = call(
            functools.partial(ends_kernel, chips),
            [part(6)] + [part(3)] * (chips - 1),
            (ends, outer, inner, end_w, own_coef),
            0.2,
        )
        others = across(parts)
        solved, *send = call(
            halo_kernel,
            [field] + ([(3, nz, half, ny)] if last else []),
            (solved, outer, inner, edge_w, ratio, recip),
            0.4,
            after=parts[:1],
            scratch=[pltpu.VMEM((3, 2, levels, ny), F32)],
        )
        more = () if last else (solved, bottom_w, top_w)
        outs = call(
            functools.partial(join_kernel, chips, not last),
            [part(6)] if last else [field, plane, plane],
            (*others, volts, below, above, own_coef, *more),
            0.4,
            scratch=[pltpu.VMEM((chips, 3, half, ny), F32)],
        )
        if not last:
            state, outer, inner = outs
    solved_other, w_other = swap(send[0]), swap(w_send)
    (currents,) = outs
    (out,) = call(
        last_kernel,
        [adjoint.shape],
        (solved, bottom_w, top_w, currents, solved_other, w_other, swap(currents)),
        1.0,
    )
    return out


def solution(mesh):
    in_specs = (
        P(None, "gz", "gx", None),
        P(None, "gz", "gx", None),
        P("gz", "gx", None),
        P("gx", None),
        P(),
        P(),
        P(),
    )
    out_specs = P(None, "gz", "gx", None)
    body = functools.partial(per_device, mesh.shape["gx"], mesh.shape["gz"])
    return jax.shard_map(body, mesh=mesh, in_specs=in_specs, out_specs=out_specs, check_vma=False)
```
